32 devices in a mesh: tm: 8 (over y, x, core), cell: 4 (over z).
Axes of the slice: x: 2, y: 2, z: 4, core: 2. Of those that a mesh axis runs over, the one named last changes fastest.
Arguments:
- theta: float32 [3, 1024, 32], P(None, 'cell', 'tm'), may hold values from -0.6 to 0.6
- tangent: float32 [3, 1024, 32], P(None, 'cell', 'tm'), may hold values from -6 to 6
- covariates: float32 [3, 2048, 4096], P(None, 'cell', 'tm'), may hold values from -4 to 4
- counts: int32 [2048, 4096], P('cell', 'tm'), may hold values from 0 to 5
- sfirst: int32 [2048], P('cell'), may hold values from 0 to 1008, as said below
- sweight: float32 [16, 2048], P(None, 'cell'), may hold values from 0.05 to 1
- tfirst: int32 [4096], P('tm'), may hold values from 0 to 28, as said below
- tweight: float32 [4, 4096], P(None, 'tm'), may hold values from 0.05 to 1
Outputs:
- hess_vec: float32 [3, 1024, 32], P(None, 'cell', 'tm')
- gradient: float32 [3, 1024, 32], P(None, 'cell', 'tm')
The draws below stay inside these ranges and needn't reach their ends.
Inputs may be any that keep to these rules, and one draw needn't show every extreme that they name: Cell c's support block sfirst[c] to sfirst[c] + 15 lies within the basis functions (c // 512) * 256 - 16 to (c // 512 + 1) * 256 + 15. Hour h's support block tfirst[h] to tfirst[h] + 3 lies within the basis functions (h // 512) * 4 - 2 to (h // 512 + 1) * 4 + 1.
All inputs are finite; a program needn't handle non-finite values.
Results may differ from the reference program's by a relative error of at most 0.0002.
Values sent between devices are 32-bit elements; how exact they have to be, the bound alone decides.
A program may use at most 64 MiB of HBM per device.

```python
import jax
import jax.numpy as jnp
from jax import lax

K = 3
S = 1024
TD = 4
WS = 16
WT = 4
HS = 16
HT = 2
CD = 512
HD = 512
TB = 32
SD = 256
NC = 2048
NH = 4096


def band_first(key, count_all, per_device, own_count, reach_back, support, limit):
    position = jnp.arange(count_all, dtype=jnp.int32)
    device = position // per_device
    lowest = jnp.maximum(device * own_count - reach_back, 0)
    highest = jnp.minimum(device * own_count + own_count + reach_back - support, limit - support)
    picked = jax.random.randint(key, (count_all,), 0, 1 << 20, dtype=jnp.int32)
    chosen = lowest + picked % (highest - lowest + 1)
    within = position % per_device
    chosen = jnp.where(within == 0, lowest, jnp.where(within == per_device - 1, highest, chosen))
    return chosen.astype(jnp.int32)


def draw_sfirst(key, part):
    return band_first(jax.random.fold_in(key, 11), NC, CD, SD, HS, WS, S)


def draw_tfirst(key, part):
    return band_first(jax.random.fold_in(key, 23), NH, HD, TD, HT, WT, TB)


def set_ends(entries, own_key, smallest, high):
    place = [jax.random.randint(jax.random.fold_in(own_key, axis), (), 0, length) for axis, length in enumerate(entries.shape)]
    longest = entries.shape.index(max(entries.shape))
    next_to = place[:longest] + [(place[longest] + 1) % entries.shape[longest]] + place[longest + 1:]
    return entries.at[tuple(place)].set(smallest).at[tuple(next_to)].set(high)


def steps_of(key, shape, shards, smallest, high):
    def one(dim, parts):
        draws = jax.random.uniform(jax.random.fold_in(jax.random.fold_in(key, 6), dim), (parts,), jnp.float32, smallest / len(shards), high / len(shards))
        return jnp.repeat(jnp.exp(draws), shape[dim] // parts).reshape((-1,) + (1,) * (len(shape) - dim - 1))

    loudness = one(*shards[0])
    for cut in shards[1:]:
        loudness = loudness * one(*cut)
    return loudness


def normal_values(stream_key, dims, deviation, most, cuts=(), held_as=jnp.bfloat16):
    drawn = deviation * jax.random.normal(stream_key, dims, jnp.float32)
    if cuts:
        drawn = drawn * steps_of(stream_key, dims, cuts, -0.22, 0.18)
    return jnp.clip(drawn, -most, most).astype(held_as)


def setup_inputs(seed: int = 0) -> dict:
    seeds = jax.random.split(jax.random.key(seed), 9)
    return {
        "theta": normal_values(seeds[0], (K, S, TB), 0.1, 0.6, ((1, 4), (2, 8)), jnp.float32),
        "tangent": normal_values(seeds[1], (K, S, TB), 1.0, 6.0, ((1, 4), (2, 8)), jnp.float32),
        "covariates": normal_values(seeds[2], (K, NC, NH), 1.0, 4.0, ((1, 4), (2, 8)), jnp.float32),
        "counts": set_ends(jax.random.randint(seeds[3], (NC, NH), 0, 6), jax.random.fold_in(seeds[3], 1), 0, 5).astype(jnp.int32),
        "sfirst": draw_sfirst(jax.random.fold_in(seeds[8], 71), 0),
        "sweight": jnp.clip(0.05 + 0.95 * jax.random.uniform(seeds[5], (WS, NC), jnp.float32) ** steps_of(seeds[5], (WS, NC), ((1, 4),), -0.2, 0.2), 0.05, 1.0),
        "tfirst": draw_tfirst(jax.random.fold_in(seeds[8], 71), 0),
        "tweight": jnp.clip(0.05 + 0.95 * jax.random.uniform(seeds[7], (WT, NH), jnp.float32) ** steps_of(seeds[7], (WT, NH), ((1, 8),), -0.2, 0.2), 0.05, 1.0),
    }


def basis_block(first, values, row_total, offset):
    diffs = jnp.arange(row_total, dtype=jnp.int32)[:, None] - (first - offset).astype(jnp.int32)[None, :]
    result = jnp.zeros((row_total, first.shape[0]), jnp.float32)
    for index in range(values.shape[0]):
        result = result + jnp.where(diffs == index, values[index][None, :], jnp.float32(0.0))
    return result


def reference(theta, tangent, covariates, counts, sfirst, sweight, tfirst, tweight):
    high = lax.Precision.HIGHEST
    space_basis = basis_block(sfirst, sweight, S, 0)
    stacked = jnp.stack([theta, tangent])
    spatial = jnp.einsum("sc,pkst->pkct", space_basis, stacked, precision=high)
    blocks = NH // HD

    def one_block(step, total):
        start = (step * HD).astype(jnp.int32)
        time_basis = basis_block(lax.dynamic_slice_in_dim(tfirst, start, HD, 0), lax.dynamic_slice_in_dim(tweight, start, HD, 1), TB, 0)
        covar_blk = lax.dynamic_slice_in_dim(covariates, start, HD, 2)
        count_blk = lax.dynamic_slice_in_dim(counts, start, HD, 1).astype(jnp.float32)
        fields = jnp.einsum("pkct,th->pkch", spatial, time_basis, precision=high)
        predictor = jnp.sum(covar_blk * fields[0], axis=0)
        tangent_pred = jnp.sum(covar_blk * fields[1], axis=0)
        rates = jnp.exp(predictor)
        weighted = jnp.stack([covar_blk * (rates * tangent_pred)[None], covar_blk * (count_blk - rates)[None]])
        return total + jnp.einsum("pkch,th->pkct", weighted, time_basis, precision=high)

    start_total = jnp.zeros((2, K, NC, TB), jnp.float32)
    time_part = lax.fori_loop(0, blocks, one_block, start_total)
    summed = jnp.einsum("sc,pkct->pkst", space_basis, time_part, precision=high)
    hess_vec = summed[0] / jnp.float32(WS * (HD // TD))
    gradient = summed[1] / jnp.float32(HD // TD)
    return hess_vec, gradient
```

```python
import functools

import jax
import jax.numpy as jnp
from jax import lax
from jax.experimental import pallas as pl
from jax.experimental.pallas import tpu as pltpu
from jax.sharding import PartitionSpec as P

HS = 16
HT = 2
LANES = 128
SUB = 8
CHUNK = 128
MESH = pl.DeviceIdType.MESH
DIRS = [(dt, dc) for dt in (1, -1, 0) for dc in (0, 1, -1) if (dt, dc) != (0, 0)]
F32 = jnp.float32
BF16 = jnp.bfloat16


def split(value):
    head = value.astype(BF16).astype(F32)
    return head, value - head


def bf16_dot(left, right):
    return lax.dot_general(left, right, (((1,), (0,)), ((), ())), preferred_element_type=F32)


def kernel(
    nt, nc, theta_h, tangent_h, covar_h, counts_h, sfirst_h, sweight_h, tfirst_h, tweight_h, out_ref,
    theta, tangent, covar, counts, sfirst, sweight, tfirst, tweight,
    own, low, high, space_head, space_rest, time_rows, time_cols, back,
    res_own, res_edge, got, load_sem, chunk_sem, send_sem, recv_sem, back_send, back_recv,
):
    covs, td, sd = theta.shape
    cd, hd = counts.shape
    te = td + 2 * HT
    rows = te * SUB
    chunks = cd // CHUNK
    me_t, me_c = lax.axis_index("tm"), lax.axis_index("cell")

    loads = []
    for i, (src, dst) in enumerate(
        [(theta_h, theta), (tangent_h, tangent), (tfirst_h, tfirst), (tweight_h, tweight), (sfirst_h, sfirst), (sweight_h, sweight)]
    ):
        loads.append(pltpu.make_async_copy(src, dst, load_sem.at[i]))
        loads[-1].start()
    chunk_loads = []
    for i in range(chunks):
        part = pl.ds(i * CHUNK, CHUNK)
        pair = (
            pltpu.make_async_copy(covar_h.at[:, part], covar.at[:, part], chunk_sem.at[0, i]),
            pltpu.make_async_copy(counts_h.at[part], counts.at[part], chunk_sem.at[1, i]),
        )
        for copy in pair:
            copy.start()
        chunk_loads.append(pair)

    def there(dt, dc):
        inside = me_t >= 0
        if dt:
            inside = jnp.logical_and(inside, (me_t < nt - 1) if dt > 0 else (me_t > 0))
        if dc:
            inside = jnp.logical_and(inside, (me_c < nc - 1) if dc > 0 else (me_c > 0))
        return inside

    def device(dt, dc):
        return {"tm": me_t + dt, "cell": me_c + dc}

    for ref in [own, low, high] + got:
        ref[...] = jnp.zeros(ref.shape, F32)
    barrier = pltpu.get_barrier_semaphore()
    for dt, dc in DIRS:
        @pl.when(there(dt, dc))
        def _(dt=dt, dc=dc):
            pl.semaphore_signal(barrier, inc=1, device_id=device(dt, dc), device_id_type=MESH)

    loads[0].wait()
    loads[1].wait()
    for p, ref in enumerate((theta, tangent)):
        for k in range(covs):
            own[0:td, p * covs + k, :] = ref[k]

    loads[2].wait()
    loads[3].wait()
    index = lax.broadcasted_iota(jnp.int32, (rows, hd), 0) // SUB
    place = jnp.where(index < td, index, jnp.where(index < td + HT, index - (td + HT), index - HT)) + me_t * td
    diffs = place - tfirst[...]
    basis = jnp.zeros((rows, hd), F32)
    for j in range(tweight.shape[0]):
        basis = jnp.where(diffs == j, tweight[j : j + 1, :], basis)
    head, rest = split(basis)
    both = jnp.concatenate([head, rest], axis=0)
    time_cols[...] = both.T.astype(BF16)
    head, rest = head.astype(BF16), rest.astype(BF16)
    time_rows[...] = jnp.concatenate([head, head, rest, rest], axis=0)

    beside_t = (me_t > 0).astype(jnp.int32) + (me_t < nt - 1).astype(jnp.int32)
    beside_c = (me_c > 0).astype(jnp.int32) + (me_c < nc - 1).astype(jnp.int32)
    pl.semaphore_wait(barrier, (beside_t + 1) * (beside_c + 1) - 1)

    def forward(i, dt, dc):
        src_t = {0: pl.ds(0, td), 1: pl.ds(td - HT, HT), -1: pl.ds(0, HT)}[dt]
        dst_t = {0: pl.ds(0, td), 1: pl.ds(td, HT), -1: pl.ds(td + HT, HT)}[dt]
        src_s = {0: pl.ds(0, sd), 1: pl.ds(sd - LANES, LANES), -1: pl.ds(0, LANES)}[dc]
        dst = {0: own, 1: low, -1: high}[dc]
        return pltpu.make_async_remote_copy(
            src_ref=own.at[src_t, :, src_s], dst_ref=dst.at[dst_t],
            send_sem=send_sem.at[i], recv_sem=recv_sem.at[i], device_id=device(dt, dc), device_id_type=MESH,
        )

    for i, (dt, dc) in enumerate(DIRS):
        @pl.when(there(dt, dc))
        def _(i=i, dt=dt, dc=dc):
            forward(i, dt, dc).start()

    loads[4].wait()
    loads[5].wait()
    first = sfirst[...]
    support = sweight.shape[0]
    taps = jnp.concatenate([sweight[...], jnp.zeros((SUB, cd), F32)], axis=0)
    shift = 1
    while shift < SUB:
        taps = jnp.where((first & shift) != 0, pltpu.roll(taps, shift, 0), taps)
        shift *= 2
    group = jnp.broadcast_to(first // SUB - me_c * (sd // SUB), (SUB, cd))
    blank = jnp.zeros((SUB, cd), F32)
    for block in range(sd // LANES + 1):
        parts = []
        for g in range(LANES // SUB):
            if block < sd // LANES:
                number = block * (LANES // SUB) + g
            elif g < HS // SUB:
                number = sd // SUB + g
            elif g >= (LANES - HS) // SUB:
                number = g - LANES // SUB
            else:
                parts.append(blank)
                continue
            part = blank
            for m in range(support // SUB + 1):
                part = jnp.where(group == number - m, taps[m * SUB : (m + 1) * SUB], part)
            parts.append(part)
        head, rest = split(jnp.concatenate(parts, axis=0).T)
        space_head[:, block * LANES : (block + 1) * LANES] = head.astype(BF16)
        space_rest[:, block * LANES : (block + 1) * LANES] = rest.astype(BF16)

    for i, (dt, dc) in enumerate(DIRS):
        @pl.when(there(-dt, -dc))
        def _(i=i, dt=dt, dc=dc):
            forward(i, dt, dc).wait_recv()

    lane = lax.broadcasted_iota(jnp.int32, (rows, LANES), 1)
    edge = jnp.where(lane < HS, high[...].reshape(rows, LANES), jnp.where(lane >= LANES - HS, low[...].reshape(rows, LANES), 0.0))
    head, rest = split(jnp.concatenate([own[...].reshape(rows, sd), edge], axis=1))
    coef = jnp.concatenate([head, rest], axis=0).astype(BF16)
    nt_dims = (((1,), (1,)), ((), ()))
    spatial = lax.dot_general(space_head[...], coef, nt_dims, preferred_element_type=F32)
    spatial = spatial + lax.dot_general(space_rest[...], coef, nt_dims, preferred_element_type=F32)
    spatial = spatial + pltpu.roll(spatial, rows, 1)
    head, rest = split(spatial)
    wide = lax.broadcasted_iota(jnp.int32, (cd, 2 * rows), 1)
    spatial = jnp.where(wide < rows, head, rest)

    lane = lax.broadcasted_iota(jnp.int32, (CHUNK, 2 * rows), 1)
    which = lane % SUB
    for i in range(chunks):
        chunk_loads[i][0].wait()
        chunk_loads[i][1].wait()
        part = slice(i * CHUNK, (i + 1) * CHUNK)
        fields = []
        for n in range(2 * covs):
            picked = jnp.where(which == n, spatial[part], 0.0).astype(BF16)
            fields.append(bf16_dot(jnp.concatenate([picked, picked], axis=1), time_rows[...]))
        predictor = covar[0, part, :] * fields[0]
        tangent_pred = covar[0, part, :] * fields[covs]
        for k in range(1, covs):
            predictor = predictor + covar[k, part, :] * fields[k]
            tangent_pred = tangent_pred + covar[k, part, :] * fields[covs + k]
        rates = jnp.exp(predictor)
        factors = (rates * tangent_pred, counts[part, :].astype(F32) - rates)
        total = jnp.zeros((CHUNK, 2 * rows), F32)
        for n in range(2 * covs):
            head, rest = split(covar[n % covs, part, :] * factors[n // covs])
            value = bf16_dot(head.astype(BF16), time_cols[...]) + bf16_dot(rest.astype(BF16), time_cols[...])
            total = jnp.where(which == n, value, total)
        total = total + pltpu.roll(total, rows, 1)
        head, rest = split(total)
        back[:, part] = jnp.where(lane < rows, head, rest).T.astype(BF16)

    result = bf16_dot(back[...], space_head[...]) + bf16_dot(back[...], space_rest[...])
    result = (result[:rows] + result[rows:]).reshape(te, SUB, sd + LANES)
    res_own[...] = result[:, :, :sd]
    res_edge[...] = result[:, :, sd:]

    def backward(i, dt, dc):
        src_t = {0: pl.ds(0, td), 1: pl.ds(td + HT, HT), -1: pl.ds(td, HT)}[dt]
        src = res_edge if dc else res_own
        return pltpu.make_async_remote_copy(
            src_ref=src.at[src_t], dst_ref=got[i],
            send_sem=back_send.at[i], recv_sem=back_recv.at[i], device_id=device(dt, dc), device_id_type=MESH,
        )

    for i, (dt, dc) in enumerate(DIRS):
        @pl.when(there(dt, dc))
        def _(i=i, dt=dt, dc=dc):
            forward(i, dt, dc).wait_send()
            backward(i, dt, dc).start()
    for i, (dt, dc) in enumerate(DIRS):
        @pl.when(there(-dt, -dc))
        def _(i=i, dt=dt, dc=dc):
            backward(i, dt, dc).wait_recv()

    lane = lax.broadcasted_iota(jnp.int32, (1, 1, LANES), 2)
    sums = [[res_own[t : t + 1, :, b * LANES : (b + 1) * LANES] for b in range(sd // LANES)] for t in range(td)]
    for i, (dt, dc) in enumerate(DIRS):
        start = td - HT if dt < 0 else 0
        for t in range(got[i].shape[0]):
            value = got[i][t : t + 1]
            if dc == 0:
                for b in range(sd // LANES):
                    sums[start + t][b] += value[:, :, b * LANES : (b + 1) * LANES]
            elif dc > 0:
                sums[start + t][0] += jnp.where(lane < HS, value, 0.0)
            else:
                sums[start + t][-1] += jnp.where(lane >= LANES - HS, value, 0.0)
    total = jnp.concatenate([jnp.concatenate(row, axis=2) for row in sums], axis=0)
    for p in range(2):
        scale = F32((sweight.shape[0] if p == 0 else 1) * (hd // td))
        for k in range(covs):
            out_ref[p, k] = total[:, p * covs + k, :] / scale

    for i, (dt, dc) in enumerate(DIRS):
        @pl.when(there(dt, dc))
        def _(i=i, dt=dt, dc=dc):
            backward(i, dt, dc).wait_send()


def body(nt, nc, theta, tangent, covariates, counts, sfirst, sweight, tfirst, tweight):
    covs, sd, td = theta.shape
    cd, hd = counts.shape
    te = td + 2 * HT
    operands = (
        theta.transpose(0, 2, 1), tangent.transpose(0, 2, 1), covariates, counts,
        sfirst.reshape(1, cd), sweight, tfirst.reshape(1, hd), tweight,
    )
    got = [
        pltpu.VMEM((HT if dt else td, SUB, LANES if dc else sd), F32) for dt, dc in DIRS
    ]
    dirs = len(DIRS)
    out = pl.pallas_call(
        functools.partial(kernel, nt, nc),
        out_shape=jax.ShapeDtypeStruct((2, covs, td, sd), F32),
        in_specs=[pl.BlockSpec(memory_space=pltpu.HBM)] * len(operands),
        out_specs=pl.BlockSpec(memory_space=pltpu.VMEM),
        scratch_shapes=[pltpu.VMEM(x.shape, x.dtype) for x in operands]
        + [
            pltpu.VMEM((te, SUB, sd), F32),
            pltpu.VMEM((te, SUB, LANES), F32),
            pltpu.VMEM((te, SUB, LANES), F32),
            pltpu.VMEM((cd, sd + LANES), BF16),
            pltpu.VMEM((cd, sd + LANES), BF16),
            pltpu.VMEM((4 * te * SUB, hd), BF16),
            pltpu.VMEM((hd, 2 * te * SUB), BF16),
            pltpu.VMEM((2 * te * SUB, cd), BF16),
            pltpu.VMEM((te, SUB, sd), F32),
            pltpu.VMEM((te, SUB, LANES), F32),
            got,
            pltpu.SemaphoreType.DMA((6,)),
            pltpu.SemaphoreType.DMA((2, cd // CHUNK)),
            pltpu.SemaphoreType.DMA((dirs,)),
            pltpu.SemaphoreType.DMA((dirs,)),
            pltpu.SemaphoreType.DMA((dirs,)),
            pltpu.SemaphoreType.DMA((dirs,)),
        ],
        compiler_params=pltpu.CompilerParams(
            collective_id=0, has_side_effects=True, vmem_limit_bytes=60 * 1024 * 1024
        ),
        name="hessian_product",
    )(*operands)
    out = out.transpose(0, 1, 3, 2)
    return out[0], out[1]


def solution(mesh):
    return jax.shard_map(
        functools.partial(body, mesh.shape["tm"], mesh.shape["cell"]),
        mesh=mesh,
        in_specs=(
            P(None, "cell", "tm"),
            P(None, "cell", "tm"),
            P(None, "cell", "tm"),
            P("cell", "tm"),
            P("cell"),
            P(None, "cell"),
            P("tm"),
            P(None, "tm"),
        ),
        out_specs=(P(None, "cell", "tm"), P(None, "cell", "tm")),
        check_vma=False,
    )
```

```python
import functools

import jax
import jax.numpy as jnp
from jax import lax
from jax.experimental import pallas as pl
from jax.experimental.pallas import tpu as pltpu
from jax.sharding import PartitionSpec as P

HS = 16
HT = 2
LANES = 128
SUB = 8
CHUNK = 128
STRIP = 16
STRIP_COLS = 256
MESH = pl.DeviceIdType.MESH
DIRS = [(dt, dc) for dt in (1, -1, 0) for dc in (0, 1, -1) if (dt, dc) != (0, 0)]
F32 = jnp.float32
BF16 = jnp.bfloat16


def split(value):
    head = value.astype(BF16)
    return head, (value - head.astype(F32)).astype(BF16)


def split_wide(value):
    head = value.astype(BF16).astype(F32)
    return head, value - head


def bf16_dot(left, right):
    return lax.dot_general(left, right, (((1,), (0,)), ((), ())), preferred_element_type=F32)


def kernel(
    nt, nc, theta_h, tangent_h, covar_h, counts_h, sfirst_h, sweight_h, tfirst_h, tweight_h, out_ref,
    theta, tangent, covar, counts, sfirst, sweight, tfirst, tweight,
    own, low, high, space_head, space_rest, time_rows, time_cols, spatial, fields, weighted, back,
    res_own, res_edge, got, load_sem, chunk_sem, send_sem, recv_sem, back_send, back_recv,
):
    covs, td, sd = theta.shape
    cd, hd = counts.shape
    te = td + 2 * HT
    rows = te * SUB
    chunks = cd // CHUNK
    me_t, me_c = lax.axis_index("tm"), lax.axis_index("cell")

    loads = [
        pltpu.make_async_copy(src, dst, load_sem.at[i])
        for i, (src, dst) in enumerate(
            [(theta_h, theta), (tangent_h, tangent), (tfirst_h, tfirst), (tweight_h, tweight), (sfirst_h, sfirst), (sweight_h, sweight)]
        )
    ]
    loads[0].start()
    loads[1].start()

    def there(dt, dc):
        inside = me_t >= 0
        if dt:
            inside = jnp.logical_and(inside, (me_t < nt - 1) if dt > 0 else (me_t > 0))
        if dc:
            inside = jnp.logical_and(inside, (me_c < nc - 1) if dc > 0 else (me_c > 0))
        return inside

    def device(dt, dc):
        return {"tm": me_t + dt, "cell": me_c + dc}

    for ref in [own, low, high] + got:
        ref[...] = jnp.zeros(ref.shape, F32)
    barrier = pltpu.get_barrier_semaphore()
    for dt, dc in DIRS:
        @pl.when(there(dt, dc))
        def _(dt=dt, dc=dc):
            pl.semaphore_signal(barrier, inc=1, device_id=device(dt, dc), device_id_type=MESH)

    for copy in loads[2:]:
        copy.start()
    chunk_loads = []
    for i in range(chunks):
        part = pl.ds(i * CHUNK, CHUNK)
        pair = (
            pltpu.make_async_copy(covar_h.at[:, part], covar.at[:, part], chunk_sem.at[0, i]),
            pltpu.make_async_copy(counts_h.at[part], counts.at[part], chunk_sem.at[1, i]),
        )
        for copy in pair:
            copy.start()
        chunk_loads.append(pair)

    loads[0].wait()
    loads[1].wait()
    for p, ref in enumerate((theta, tangent)):
        for k in range(covs):
            own[0:td, p * covs + k, :] = ref[k]

    beside_t = (me_t > 0).astype(jnp.int32) + (me_t < nt - 1).astype(jnp.int32)
    beside_c = (me_c > 0).astype(jnp.int32) + (me_c < nc - 1).astype(jnp.int32)
    pl.semaphore_wait(barrier, (beside_t + 1) * (beside_c + 1) - 1)

    def forward(i, dt, dc):
        src_t = {0: pl.ds(0, td), 1: pl.ds(td - HT, HT), -1: pl.ds(0, HT)}[dt]
        dst_t = {0: pl.ds(0, td), 1: pl.ds(td, HT), -1: pl.ds(td + HT, HT)}[dt]
        src_s = {0: pl.ds(0, sd), 1: pl.ds(sd - LANES, LANES), -1: pl.ds(0, LANES)}[dc]
        dst = {0: own, 1: low, -1: high}[dc]
        return pltpu.make_async_remote_copy(
            src_ref=own.at[src_t, :, src_s], dst_ref=dst.at[dst_t],
            send_sem=send_sem.at[i], recv_sem=recv_sem.at[i], device_id=device(dt, dc), device_id_type=MESH,
        )

    for i, (dt, dc) in enumerate(DIRS):
        @pl.when(there(dt, dc))
        def _(i=i, dt=dt, dc=dc):
            forward(i, dt, dc).start()

    loads[2].wait()
    loads[3].wait()
    index = lax.broadcasted_iota(jnp.int32, (rows, hd), 0) // SUB
    place = jnp.where(index < td, index, jnp.where(index < td + HT, index - (td + HT), index - HT)) + me_t * td
    diffs = place - tfirst[...]
    basis = jnp.zeros((rows, hd), F32)
    for j in range(tweight.shape[0]):
        basis = jnp.where(diffs == j, tweight[j : j + 1, :], basis)
    head, rest = split_wide(basis)
    turned = jnp.concatenate([head, rest], axis=0).T.astype(BF16)
    time_cols[...] = jnp.concatenate([turned, turned], axis=0)
    head, rest = head.astype(BF16), rest.astype(BF16)
    time_rows[...] = jnp.concatenate([head, head, rest, rest], axis=0)

    loads[4].wait()
    loads[5].wait()
    first = sfirst[...]
    support = sweight.shape[0]
    taps = jnp.concatenate([sweight[...], jnp.zeros((SUB, cd), F32)], axis=0)
    shift = 1
    while shift < SUB:
        taps = jnp.where((first & shift) != 0, pltpu.roll(taps, shift, 0), taps)
        shift *= 2
    group = jnp.broadcast_to(first // SUB - me_c * (sd // SUB), (SUB, cd))
    blank = jnp.zeros((SUB, cd), F32)
    for block in range(sd // LANES + 1):
        parts = []
        for g in range(LANES // SUB):
            if block < sd // LANES:
                number = block * (LANES // SUB) + g
            elif g < HS // SUB:
                number = sd // SUB + g
            elif g >= (LANES - HS) // SUB:
                number = g - LANES // SUB
            else:
                parts.append(blank)
                continue
            part = blank
            for m in range(support // SUB + 1):
                part = jnp.where(group == number - m, taps[m * SUB : (m + 1) * SUB], part)
            parts.append(part)
        head, rest = split(jnp.concatenate(parts, axis=0).T)
        space_head[:, block * LANES : (block + 1) * LANES] = head
        space_rest[:, block * LANES : (block + 1) * LANES] = rest

    for i, (dt, dc) in enumerate(DIRS):
        @pl.when(there(-dt, -dc))
        def _(i=i, dt=dt, dc=dc):
            forward(i, dt, dc).wait_recv()

    lane = lax.broadcasted_iota(jnp.int32, (rows, LANES), 1)
    edge = jnp.where(lane < HS, high[...].reshape(rows, LANES), jnp.where(lane >= LANES - HS, low[...].reshape(rows, LANES), 0.0))
    head, rest = split(jnp.concatenate([own[...].reshape(rows, sd), edge], axis=1))
    coef = jnp.concatenate([head, rest], axis=0)
    nt_dims = (((1,), (1,)), ((), ()))
    value = lax.dot_general(space_head[...], coef, nt_dims, preferred_element_type=F32)
    value = value + lax.dot_general(space_rest[...], coef, nt_dims, preferred_element_type=F32)
    value = value + pltpu.roll(value, rows, 1)
    head, rest = split_wide(value)
    wide = lax.broadcasted_iota(jnp.int32, (cd, 2 * rows), 1)
    spatial[...] = jnp.where(wide < rows, head, rest)

    lane = lax.broadcasted_iota(jnp.int32, (CHUNK, 2 * rows), 1)
    which = lane % SUB

    def fields_of(i):
        value = spatial[i * CHUNK : (i + 1) * CHUNK, :]
        picked = [jnp.where(which == n, value, 0.0).astype(BF16) for n in range(2 * covs)]
        picked = jnp.concatenate(picked, axis=0)
        fields[i % 2] = bf16_dot(jnp.concatenate([picked, picked], axis=1), time_rows[...])

    def weigh(i):
        for r in range(0, CHUNK, STRIP):
            for c in range(0, hd, STRIP_COLS):
                cells = slice(i * CHUNK + r, i * CHUNK + r + STRIP)
                hours = slice(c, c + STRIP_COLS)
                cov = [covar[k, cells, hours] for k in range(covs)]

                def field(n):
                    return fields[i % 2, n * CHUNK + r : n * CHUNK + r + STRIP, hours]

                predictor = cov[0] * field(0)
                tangent_pred = cov[0] * field(covs)
                for k in range(1, covs):
                    predictor = predictor + cov[k] * field(k)
                    tangent_pred = tangent_pred + cov[k] * field(covs + k)
                rates = jnp.exp(predictor)
                factors = (rates * tangent_pred, counts[cells, hours].astype(F32) - rates)
                for n in range(2 * covs):
                    head, rest = split(cov[n % covs] * factors[n // covs])
                    place = slice(n * CHUNK + r, n * CHUNK + r + STRIP)
                    weighted[i % 2, place, c : c + STRIP_COLS] = head
                    weighted[i % 2, place, hd + c : hd + c + STRIP_COLS] = rest

    def sums_of(i):
        value = bf16_dot(weighted[i % 2], time_cols[...])
        total = value[:CHUNK]
        for n in range(1, 2 * covs):
            total = jnp.where(which == n, value[n * CHUNK : (n + 1) * CHUNK], total)
        total = jnp.where(which < 2 * covs, total, 0.0)
        total = total + pltpu.roll(total, rows, 1)
        head, rest = split_wide(total)
        back[:, i * CHUNK : (i + 1) * CHUNK] = jnp.where(lane < rows, head, rest).T.astype(BF16)

    fields_of(0)
    for i in range(chunks):
        chunk_loads[i][0].wait()
        chunk_loads[i][1].wait()
        if i + 1 < chunks:
            fields_of(i + 1)
        weigh(i)
        sums_of(i)

    def backward(i, dt, dc):
        src_t = {0: pl.ds(0, td), 1: pl.ds(td + HT, HT), -1: pl.ds(td, HT)}[dt]
        src = res_edge if dc else res_own
        return pltpu.make_async_remote_copy(
            src_ref=src.at[src_t], dst_ref=got[i],
            send_sem=back_send.at[i], recv_sem=back_recv.at[i], device_id=device(dt, dc), device_id_type=MESH,
        )

    for edges in (True, False):
        columns = slice(sd, sd + LANES) if edges else slice(0, sd)
        result = bf16_dot(back[...], space_head[:, columns]) + bf16_dot(back[...], space_rest[:, columns])
        result = result[:rows] + result[rows:]
        (res_edge if edges else res_own)[...] = result.reshape(te, SUB, LANES if edges else sd)
        for i, (dt, dc) in enumerate(DIRS):
            if (dc != 0) == edges:
                @pl.when(there(dt, dc))
                def _(i=i, dt=dt, dc=dc):
                    backward(i, dt, dc).start()
    for i, (dt, dc) in enumerate(DIRS):
        @pl.when(there(-dt, -dc))
        def _(i=i, dt=dt, dc=dc):
            backward(i, dt, dc).wait_recv()

    lane = lax.broadcasted_iota(jnp.int32, (1, 1, LANES), 2)
    sums = [[res_own[t : t + 1, :, b * LANES : (b + 1) * LANES] for b in range(sd // LANES)] for t in range(td)]
    for i, (dt, dc) in enumerate(DIRS):
        start = td - HT if dt < 0 else 0
        for t in range(got[i].shape[0]):
            value = got[i][t : t + 1]
            if dc == 0:
                for b in range(sd // LANES):
                    sums[start + t][b] += value[:, :, b * LANES : (b + 1) * LANES]
            elif dc > 0:
                sums[start + t][0] += jnp.where(lane < HS, value, 0.0)
            else:
                sums[start + t][-1] += jnp.where(lane >= LANES - HS, value, 0.0)
    total = jnp.concatenate([jnp.concatenate(row, axis=2) for row in sums], axis=0)
    for p in range(2):
        scale = F32((sweight.shape[0] if p == 0 else 1) * (hd // td))
        for k in range(covs):
            out_ref[p, k] = total[:, p * covs + k, :] / scale

    for i, (dt, dc) in enumerate(DIRS):
        @pl.when(there(dt, dc))
        def _(i=i, dt=dt, dc=dc):
            forward(i, dt, dc).wait_send()
            backward(i, dt, dc).wait_send()


def body(nt, nc, theta, tangent, covariates, counts, sfirst, sweight, tfirst, tweight):
    covs, sd, td = theta.shape
    cd, hd = counts.shape
    te = td + 2 * HT
    operands = (
        theta.transpose(0, 2, 1), tangent.transpose(0, 2, 1), covariates, counts,
        sfirst.reshape(1, cd), sweight, tfirst.reshape(1, hd), tweight,
    )
    got = [
        pltpu.VMEM((HT if dt else td, SUB, LANES if dc else sd), F32) for dt, dc in DIRS
    ]
    dirs = len(DIRS)
    out = pl.pallas_call(
        functools.partial(kernel, nt, nc),
        out_shape=jax.ShapeDtypeStruct((2, covs, td, sd), F32),
        in_specs=[pl.BlockSpec(memory_space=pltpu.HBM)] * len(operands),
        out_specs=pl.BlockSpec(memory_space=pltpu.VMEM),
        scratch_shapes=[pltpu.VMEM(x.shape, x.dtype) for x in operands]
        + [
            pltpu.VMEM((te, SUB, sd), F32),
            pltpu.VMEM((te, SUB, LANES), F32),
            pltpu.VMEM((te, SUB, LANES), F32),
            pltpu.VMEM((cd, sd + LANES), BF16),
            pltpu.VMEM((cd, sd + LANES), BF16),
            pltpu.VMEM((4 * te * SUB, hd), BF16),
            pltpu.VMEM((2 * hd, 2 * te * SUB), BF16),
            pltpu.VMEM((cd, 2 * te * SUB), F32),
            pltpu.VMEM((2, 2 * covs * CHUNK, hd), F32),
            pltpu.VMEM((2, 2 * covs * CHUNK, 2 * hd), BF16),
            pltpu.VMEM((2 * te * SUB, cd), BF16),
            pltpu.VMEM((te, SUB, sd), F32),
            pltpu.VMEM((te, SUB, LANES), F32),
            got,
            pltpu.SemaphoreType.DMA((6,)),
            pltpu.SemaphoreType.DMA((2, cd // CHUNK)),
            pltpu.SemaphoreType.DMA((dirs,)),
            pltpu.SemaphoreType.DMA((dirs,)),
            pltpu.SemaphoreType.DMA((dirs,)),
            pltpu.SemaphoreType.DMA((dirs,)),
        ],
        compiler_params=pltpu.CompilerParams(
            collective_id=0, has_side_effects=True, vmem_limit_bytes=60 * 1024 * 1024
        ),
        name="hessian_product",
    )(*operands)
    out = out.transpose(0, 1, 3, 2)
    return out[0], out[1]


def solution(mesh):
    return jax.shard_map(
        functools.partial(body, mesh.shape["tm"], mesh.shape["cell"]),
        mesh=mesh,
        in_specs=(
            P(None, "cell", "tm"),
            P(None, "cell", "tm"),
            P(None, "cell", "tm"),
            P("cell", "tm"),
            P("cell"),
            P(None, "cell"),
            P("tm"),
            P(None, "tm"),
        ),
        out_specs=(P(None, "cell", "tm"), P(None, "cell", "tm")),
        check_vma=False,
    )
```

```python
import functools

import jax
import jax.numpy as jnp
from jax import lax
from jax.experimental import pallas as pl
from jax.experimental.pallas import tpu as pltpu
from jax.sharding import PartitionSpec as P

HS = 16
HT = 2
LANES = 128
SUB = 8
CHUNK = 128
MESH = pl.DeviceIdType.MESH
DIRS = [(dt, dc) for dt in (1, -1, 0) for dc in (0, 1, -1) if (dt, dc) != (0, 0)]
F32 = jnp.float32
BF16 = jnp.bfloat16


def split(value):
    head = value.astype(BF16)
    return head, (value - head.astype(F32)).astype(BF16)


def split_wide(value):
    head = value.astype(BF16).astype(F32)
    return head, value - head


def bf16_dot(left, right):
    return lax.dot_general(left, right, (((1,), (0,)), ((), ())), preferred_element_type=F32)


def kernel(
    nt, nc, theta_h, tangent_h, covar_h, counts_h, sfirst_h, sweight_h, tfirst_h, tweight_h, out_ref,
    theta, tangent, covar, counts, sfirst, sweight, tfirst, tweight,
    own, low, high, space_head, space_rest, time_rows, time_cols, back,
    res_own, res_edge, got, load_sem, send_sem, recv_sem, back_send, back_recv,
):
    covs, td, sd = theta.shape
    cd, hd = counts.shape
    te = td + 2 * HT
    rows = te * SUB
    me_t, me_c = lax.axis_index("tm"), lax.axis_index("cell")

    loads = [
        pltpu.make_async_copy(src, dst, load_sem.at[i])
        for i, (src, dst) in enumerate(
            [(theta_h, theta), (tangent_h, tangent), (tfirst_h, tfirst), (tweight_h, tweight), (sfirst_h, sfirst), (sweight_h, sweight)]
        )
    ]
    loads[0].start()
    loads[1].start()

    def there(dt, dc):
        inside = me_t >= 0
        if dt:
            inside = jnp.logical_and(inside, (me_t < nt - 1) if dt > 0 else (me_t > 0))
        if dc:
            inside = jnp.logical_and(inside, (me_c < nc - 1) if dc > 0 else (me_c > 0))
        return inside

    def device(dt, dc):
        return {"tm": me_t + dt, "cell": me_c + dc}

    for ref in [own, low, high] + got:
        ref[...] = jnp.zeros(ref.shape, F32)
    barrier = pltpu.get_barrier_semaphore()
    for dt, dc in DIRS:
        @pl.when(there(dt, dc))
        def _(dt=dt, dc=dc):
            pl.semaphore_signal(barrier, inc=1, device_id=device(dt, dc), device_id_type=MESH)

    for copy in loads[2:]:
        copy.start()
    chunk_loads = [
        pltpu.make_async_copy(covar_h, covar, load_sem.at[6]),
        pltpu.make_async_copy(counts_h, counts, load_sem.at[7]),
    ]
    for copy in chunk_loads:
        copy.start()

    loads[0].wait()
    loads[1].wait()
    for p, ref in enumerate((theta, tangent)):
        for k in range(covs):
            own[0:td, p * covs + k, :] = ref[k]

    beside_t = (me_t > 0).astype(jnp.int32) + (me_t < nt - 1).astype(jnp.int32)
    beside_c = (me_c > 0).astype(jnp.int32) + (me_c < nc - 1).astype(jnp.int32)
    pl.semaphore_wait(barrier, (beside_t + 1) * (beside_c + 1) - 1)

    def forward(i, dt, dc):
        src_t = {0: pl.ds(0, td), 1: pl.ds(td - HT, HT), -1: pl.ds(0, HT)}[dt]
        dst_t = {0: pl.ds(0, td), 1: pl.ds(td, HT), -1: pl.ds(td + HT, HT)}[dt]
        src_s = {0: pl.ds(0, sd), 1: pl.ds(sd - LANES, LANES), -1: pl.ds(0, LANES)}[dc]
        dst = {0: own, 1: low, -1: high}[dc]
        return pltpu.make_async_remote_copy(
            src_ref=own.at[src_t, :, src_s], dst_ref=dst.at[dst_t],
            send_sem=send_sem.at[i], recv_sem=recv_sem.at[i], device_id=device(dt, dc), device_id_type=MESH,
        )

    for i, (dt, dc) in enumerate(DIRS):
        @pl.when(there(dt, dc))
        def _(i=i, dt=dt, dc=dc):
            forward(i, dt, dc).start()

    loads[2].wait()
    loads[3].wait()
    index = lax.broadcasted_iota(jnp.int32, (rows, hd), 0) // SUB
    place = jnp.where(index < td, index, jnp.where(index < td + HT, index - (td + HT), index - HT)) + me_t * td
    diffs = place - tfirst[...]
    basis = jnp.zeros((rows, hd), F32)
    for j in range(tweight.shape[0]):
        basis = jnp.where(diffs == j, tweight[j : j + 1, :], basis)
    head, rest = split_wide(basis)
    turned = jnp.concatenate([head, rest], axis=0).T.astype(BF16)
    time_cols[...] = turned
    head, rest = head.astype(BF16), rest.astype(BF16)
    time_rows[...] = jnp.concatenate([head, head, rest, rest], axis=0)

    loads[4].wait()
    loads[5].wait()
    first = sfirst[...]
    support = sweight.shape[0]
    taps = jnp.concatenate([sweight[...], jnp.zeros((SUB, cd), F32)], axis=0)
    shift = 1
    while shift < SUB:
        taps = jnp.where((first & shift) != 0, pltpu.roll(taps, shift, 0), taps)
        shift *= 2
    group = jnp.broadcast_to(first // SUB - me_c * (sd // SUB), (SUB, cd))
    blank = jnp.zeros((SUB, cd), F32)
    for block in range(sd // LANES + 1):
        parts = []
        for g in range(LANES // SUB):
            if block < sd // LANES:
                number = block * (LANES // SUB) + g
            elif g < HS // SUB:
                number = sd // SUB + g
            elif g >= (LANES - HS) // SUB:
                number = g - LANES // SUB
            else:
                parts.append(blank)
                continue
            part = blank
            for m in range(support // SUB + 1):
                part = jnp.where(group == number - m, taps[m * SUB : (m + 1) * SUB], part)
            parts.append(part)
        head, rest = split(jnp.concatenate(parts, axis=0).T)
        space_head[:, block * LANES : (block + 1) * LANES] = head
        space_rest[:, block * LANES : (block + 1) * LANES] = rest

    for i, (dt, dc) in enumerate(DIRS):
        @pl.when(there(-dt, -dc))
        def _(i=i, dt=dt, dc=dc):
            forward(i, dt, dc).wait_recv()

    lane = lax.broadcasted_iota(jnp.int32, (rows, LANES), 1)
    edge = jnp.where(lane < HS, high[...].reshape(rows, LANES), jnp.where(lane >= LANES - HS, low[...].reshape(rows, LANES), 0.0))
    head, rest = split(jnp.concatenate([own[...].reshape(rows, sd), edge], axis=1))
    coef = jnp.concatenate([head, rest], axis=0)
    nt_dims = (((1,), (1,)), ((), ()))
    value = lax.dot_general(space_head[...], coef, nt_dims, preferred_element_type=F32)
    value = value + lax.dot_general(space_rest[...], coef, nt_dims, preferred_element_type=F32)
    value = value + pltpu.roll(value, rows, 1)
    head, rest = split_wide(value)
    wide = lax.broadcasted_iota(jnp.int32, (cd, 2 * rows), 1)
    spatial = jnp.where(wide < rows, head, rest)

    for copy in chunk_loads:
        copy.wait()
    lane = lax.broadcasted_iota(jnp.int32, (CHUNK, 2 * rows), 1)
    which = lane % SUB
    for start in range(0, cd, CHUNK):
        part = slice(start, start + CHUNK)
        fields = []
        for n in range(2 * covs):
            picked = jnp.where(which == n, spatial[part], 0.0).astype(BF16)
            fields.append(bf16_dot(jnp.concatenate([picked, picked], axis=1), time_rows[...]))
        predictor = covar[0, part, :] * fields[0]
        tangent_pred = covar[0, part, :] * fields[covs]
        for k in range(1, covs):
            predictor = predictor + covar[k, part, :] * fields[k]
            tangent_pred = tangent_pred + covar[k, part, :] * fields[covs + k]
        rates = jnp.exp(predictor)
        factors = (rates * tangent_pred, counts[part, :].astype(F32) - rates)
        total = jnp.zeros((CHUNK, 2 * rows), F32)
        for n in range(2 * covs):
            head, rest = split(covar[n % covs, part, :] * factors[n // covs])
            value = bf16_dot(head, time_cols[...]) + bf16_dot(rest, time_cols[...])
            total = jnp.where(which == n, value, total)
        total = total + pltpu.roll(total, rows, 1)
        head, rest = split_wide(total)
        back[:, part] = jnp.where(lane < rows, head, rest).T.astype(BF16)

    def backward(i, dt, dc):
        src_t = {0: pl.ds(0, td), 1: pl.ds(td + HT, HT), -1: pl.ds(td, HT)}[dt]
        src = res_edge if dc else res_own
        return pltpu.make_async_remote_copy(
            src_ref=src.at[src_t], dst_ref=got[i],
            send_sem=back_send.at[i], recv_sem=back_recv.at[i], device_id=device(dt, dc), device_id_type=MESH,
        )

    for edges in (True, False):
        columns = slice(sd, sd + LANES) if edges else slice(0, sd)
        result = bf16_dot(back[...], space_head[:, columns]) + bf16_dot(back[...], space_rest[:, columns])
        result = result[:rows] + result[rows:]
        (res_edge if edges else res_own)[...] = result.reshape(te, SUB, LANES if edges else sd)
        for i, (dt, dc) in enumerate(DIRS):
            if (dc != 0) == edges:
                @pl.when(there(dt, dc))
                def _(i=i, dt=dt, dc=dc):
                    backward(i, dt, dc).start()
    for i, (dt, dc) in enumerate(DIRS):
        @pl.when(there(-dt, -dc))
        def _(i=i, dt=dt, dc=dc):
            backward(i, dt, dc).wait_recv()

    lane = lax.broadcasted_iota(jnp.int32, (1, 1, LANES), 2)
    sums = [[res_own[t : t + 1, :, b * LANES : (b + 1) * LANES] for b in range(sd // LANES)] for t in range(td)]
    for i, (dt, dc) in enumerate(DIRS):
        start = td - HT if dt < 0 else 0
        for t in range(got[i].shape[0]):
            value = got[i][t : t + 1]
            if dc == 0:
                for b in range(sd // LANES):
                    sums[start + t][b] += value[:, :, b * LANES : (b + 1) * LANES]
            elif dc > 0:
                sums[start + t][0] += jnp.where(lane < HS, value, 0.0)
            else:
                sums[start + t][-1] += jnp.where(lane >= LANES - HS, value, 0.0)
    total = jnp.concatenate([jnp.concatenate(row, axis=2) for row in sums], axis=0)
    for p in range(2):
        scale = F32((sweight.shape[0] if p == 0 else 1) * (hd // td))
        for k in range(covs):
            out_ref[p, k] = total[:, p * covs + k, :] / scale

    for i, (dt, dc) in enumerate(DIRS):
        @pl.when(there(dt, dc))
        def _(i=i, dt=dt, dc=dc):
            forward(i, dt, dc).wait_send()
            backward(i, dt, dc).wait_send()


def body(nt, nc, theta, tangent, covariates, counts, sfirst, sweight, tfirst, tweight):
    covs, sd, td = theta.shape
    cd, hd = counts.shape
    te = td + 2 * HT
    operands = (
        theta.transpose(0, 2, 1), tangent.transpose(0, 2, 1), covariates, counts,
        sfirst.reshape(1, cd), sweight, tfirst.reshape(1, hd), tweight,
    )
    got = [
        pltpu.VMEM((HT if dt else td, SUB, LANES if dc else sd), F32) for dt, dc in DIRS
    ]
    dirs = len(DIRS)
    out = pl.pallas_call(
        functools.partial(kernel, nt, nc),
        out_shape=jax.ShapeDtypeStruct((2, covs, td, sd), F32),
        in_specs=[pl.BlockSpec(memory_space=pltpu.HBM)] * len(operands),
        out_specs=pl.BlockSpec(memory_space=pltpu.VMEM),
        scratch_shapes=[pltpu.VMEM(x.shape, x.dtype) for x in operands]
        + [
            pltpu.VMEM((te, SUB, sd), F32),
            pltpu.VMEM((te, SUB, LANES), F32),
            pltpu.VMEM((te, SUB, LANES), F32),
            pltpu.VMEM((cd, sd + LANES), BF16),
            pltpu.VMEM((cd, sd + LANES), BF16),
            pltpu.VMEM((4 * te * SUB, hd), BF16),
            pltpu.VMEM((hd, 2 * te * SUB), BF16),
            pltpu.VMEM((2 * te * SUB, cd), BF16),
            pltpu.VMEM((te, SUB, sd), F32),
            pltpu.VMEM((te, SUB, LANES), F32),
            got,
            pltpu.SemaphoreType.DMA((8,)),
            pltpu.SemaphoreType.DMA((dirs,)),
            pltpu.SemaphoreType.DMA((dirs,)),
            pltpu.SemaphoreType.DMA((dirs,)),
            pltpu.SemaphoreType.DMA((dirs,)),
        ],
        compiler_params=pltpu.CompilerParams(
            collective_id=0, has_side_effects=True, vmem_limit_bytes=60 * 1024 * 1024
        ),
        name="hessian_product",
    )(*operands)
    out = out.transpose(0, 1, 3, 2)
    return out[0], out[1]


def solution(mesh):
    return jax.shard_map(
        functools.partial(body, mesh.shape["tm"], mesh.shape["cell"]),
        mesh=mesh,
        in_specs=(
            P(None, "cell", "tm"),
            P(None, "cell", "tm"),
            P(None, "cell", "tm"),
            P("cell", "tm"),
            P("cell"),
            P(None, "cell"),
            P("tm"),
            P(None, "tm"),
        ),
        out_specs=(P(None, "cell", "tm"), P(None, "cell", "tm")),
        check_vma=False,
    )
```

```python
import functools

import jax
import jax.numpy as jnp
from jax import lax
from jax.experimental import pallas as pl
from jax.experimental.pallas import tpu as pltpu
from jax.sharding import PartitionSpec as P

HS = 16
HT = 2
LANES = 128
SUB = 8
CHUNK = 256
MESH = pl.DeviceIdType.MESH
DIRS = [(dt, dc) for dt in (1, -1, 0) for dc in (0, 1, -1) if (dt, dc) != (0, 0)]
F32 = jnp.float32
BF16 = jnp.bfloat16


def split(value):
    head = value.astype(BF16)
    return head, (value - head.astype(F32)).astype(BF16)


def split_wide(value):
    head = value.astype(BF16).astype(F32)
    return head, value - head


def bf16_dot(left, right):
    return lax.dot_general(left, right, (((1,), (0,)), ((), ())), preferred_element_type=F32)


def kernel(
    nt, nc, theta_h, tangent_h, covar_h, counts_h, sfirst_h, sweight_h, tfirst_h, tweight_h, out_ref,
    theta, tangent, covar, counts, sfirst, sweight, tfirst, tweight,
    own, low, high, space, time_rows, time_cols, back,
    res_own, res_edge, got, load_sem, send_sem, recv_sem, back_send, back_recv,
):
    covs, td, sd = theta.shape
    cd, hd = counts.shape
    te = td + 2 * HT
    rows = te * SUB
    me_t, me_c = lax.axis_index("tm"), lax.axis_index("cell")

    loads = [
        pltpu.make_async_copy(src, dst, load_sem.at[i])
        for i, (src, dst) in enumerate(
            [(theta_h, theta), (tangent_h, tangent), (tfirst_h, tfirst), (tweight_h, tweight), (sfirst_h, sfirst), (sweight_h, sweight)]
        )
    ]
    loads[0].start()
    loads[1].start()

    def there(dt, dc):
        inside = me_t >= 0
        if dt:
            inside = jnp.logical_and(inside, (me_t < nt - 1) if dt > 0 else (me_t > 0))
        if dc:
            inside = jnp.logical_and(inside, (me_c < nc - 1) if dc > 0 else (me_c > 0))
        return inside

    def device(dt, dc):
        return {"tm": me_t + dt, "cell": me_c + dc}

    for ref in [own, low, high] + got:
        ref[...] = jnp.zeros(ref.shape, F32)
    barrier = pltpu.get_barrier_semaphore()
    for dt, dc in DIRS:
        @pl.when(there(dt, dc))
        def _(dt=dt, dc=dc):
            pl.semaphore_signal(barrier, inc=1, device_id=device(dt, dc), device_id_type=MESH)

    for copy in loads[2:]:
        copy.start()
    chunk_loads = [
        pltpu.make_async_copy(covar_h, covar, load_sem.at[6]),
        pltpu.make_async_copy(counts_h, counts, load_sem.at[7]),
    ]
    for copy in chunk_loads:
        copy.start()

    loads[0].wait()
    loads[1].wait()
    for p, ref in enumerate((theta, tangent)):
        for k in range(covs):
            own[0:td, p * covs + k, :] = ref[k]

    beside_t = (me_t > 0).astype(jnp.int32) + (me_t < nt - 1).astype(jnp.int32)
    beside_c = (me_c > 0).astype(jnp.int32) + (me_c < nc - 1).astype(jnp.int32)
    pl.semaphore_wait(barrier, (beside_t + 1) * (beside_c + 1) - 1)

    def forward(i, dt, dc):
        src_t = {0: pl.ds(0, td), 1: pl.ds(td - HT, HT), -1: pl.ds(0, HT)}[dt]
        dst_t = {0: pl.ds(0, td), 1: pl.ds(td, HT), -1: pl.ds(td + HT, HT)}[dt]
        src_s = {0: pl.ds(0, sd), 1: pl.ds(sd - LANES, LANES), -1: pl.ds(0, LANES)}[dc]
        dst = {0: own, 1: low, -1: high}[dc]
        return pltpu.make_async_remote_copy(
            src_ref=own.at[src_t, :, src_s], dst_ref=dst.at[dst_t],
            send_sem=send_sem.at[i], recv_sem=recv_sem.at[i], device_id=device(dt, dc), device_id_type=MESH,
        )

    for i, (dt, dc) in enumerate(DIRS):
        @pl.when(there(dt, dc))
        def _(i=i, dt=dt, dc=dc):
            forward(i, dt, dc).start()

    loads[2].wait()
    loads[3].wait()
    index = lax.broadcasted_iota(jnp.int32, (rows, hd), 0) // SUB
    place = jnp.where(index < td, index, jnp.where(index < td + HT, index - (td + HT), index - HT)) + me_t * td
    diffs = place - tfirst[...]
    basis = jnp.zeros((rows, hd), F32)
    for j in range(tweight.shape[0]):
        basis = jnp.where(diffs == j, tweight[j : j + 1, :], basis)
    head, rest = split_wide(basis)
    turned = jnp.concatenate([head, rest], axis=0).T.astype(BF16)
    time_cols[...] = turned
    head, rest = head.astype(BF16), rest.astype(BF16)
    time_rows[...] = jnp.concatenate([head, head, rest, rest], axis=0)

    loads[4].wait()
    loads[5].wait()
    first = sfirst[...]
    support = sweight.shape[0]
    taps = jnp.concatenate([sweight[...], jnp.zeros((SUB, cd), F32)], axis=0)
    shift = 1
    while shift < SUB:
        taps = jnp.where((first & shift) != 0, pltpu.roll(taps, shift, 0), taps)
        shift *= 2
    group = jnp.broadcast_to(first // SUB - me_c * (sd // SUB), (SUB, cd))
    blank = jnp.zeros((SUB, cd), F32)
    for block in range(sd // LANES + 1):
        parts = []
        for g in range(LANES // SUB):
            if block < sd // LANES:
                number = block * (LANES // SUB) + g
            elif g < HS // SUB:
                number = sd // SUB + g
            elif g >= (LANES - HS) // SUB:
                number = g - LANES // SUB
            else:
                parts.append(blank)
                continue
            part = blank
            for m in range(support // SUB + 1):
                part = jnp.where(group == number - m, taps[m * SUB : (m + 1) * SUB], part)
            parts.append(part)
        head, rest = split(jnp.concatenate(parts, axis=0).T)
        space[:cd, block * LANES : (block + 1) * LANES] = head
        space[cd:, block * LANES : (block + 1) * LANES] = rest

    for i, (dt, dc) in enumerate(DIRS):
        @pl.when(there(-dt, -dc))
        def _(i=i, dt=dt, dc=dc):
            forward(i, dt, dc).wait_recv()

    lane = lax.broadcasted_iota(jnp.int32, (rows, LANES), 1)
    edge = jnp.where(lane < HS, high[...].reshape(rows, LANES), jnp.where(lane >= LANES - HS, low[...].reshape(rows, LANES), 0.0))
    head, rest = split(jnp.concatenate([own[...].reshape(rows, sd), edge], axis=1))
    coef = jnp.concatenate([head, rest], axis=0)
    nt_dims = (((1,), (1,)), ((), ()))
    value = lax.dot_general(space[...], coef, nt_dims, preferred_element_type=F32)
    value = value[:cd] + value[cd:]
    value = value + pltpu.roll(value, rows, 1)
    head, rest = split_wide(value)
    wide = lax.broadcasted_iota(jnp.int32, (cd, 2 * rows), 1)
    spatial = jnp.where(wide < rows, head, rest)

    for copy in chunk_loads:
        copy.wait()
    lane = lax.broadcasted_iota(jnp.int32, (CHUNK, 2 * rows), 1)
    which = lane % SUB
    for start in range(0, cd, CHUNK):
        part = slice(start, start + CHUNK)
        fields = []
        for n in range(2 * covs):
            picked = jnp.where(which == n, spatial[part], 0.0).astype(BF16)
            fields.append(bf16_dot(jnp.concatenate([picked, picked], axis=1), time_rows[...]))
        predictor = covar[0, part, :] * fields[0]
        tangent_pred = covar[0, part, :] * fields[covs]
        for k in range(1, covs):
            predictor = predictor + covar[k, part, :] * fields[k]
            tangent_pred = tangent_pred + covar[k, part, :] * fields[covs + k]
        rates = jnp.exp(predictor)
        factors = (rates * tangent_pred, counts[part, :].astype(F32) - rates)
        total = jnp.zeros((CHUNK, 2 * rows), F32)
        for n in range(2 * covs):
            head, rest = split(covar[n % covs, part, :] * factors[n // covs])
            value = bf16_dot(jnp.concatenate([head, rest], axis=0), time_cols[...])
            total = jnp.where(which == n, value[:CHUNK] + value[CHUNK:], total)
        total = total + pltpu.roll(total, rows, 1)
        head, rest = split_wide(total)
        back[:, part] = jnp.where(lane < rows, head, rest).T.astype(BF16)

    def backward(i, dt, dc):
        src_t = {0: pl.ds(0, td), 1: pl.ds(td + HT, HT), -1: pl.ds(td, HT)}[dt]
        src = res_edge if dc else res_own
        return pltpu.make_async_remote_copy(
            src_ref=src.at[src_t], dst_ref=got[i],
            send_sem=back_send.at[i], recv_sem=back_recv.at[i], device_id=device(dt, dc), device_id_type=MESH,
        )

    for edges in (True, False):
        columns = slice(sd, sd + LANES) if edges else slice(0, sd)
        result = bf16_dot(jnp.concatenate([back[...], back[...]], axis=1), space[:, columns])
        result = result[:rows] + result[rows:]
        (res_edge if edges else res_own)[...] = result.reshape(te, SUB, LANES if edges else sd)
        for i, (dt, dc) in enumerate(DIRS):
            if (dc != 0) == edges:
                @pl.when(there(dt, dc))
                def _(i=i, dt=dt, dc=dc):
                    backward(i, dt, dc).start()
    for i, (dt, dc) in enumerate(DIRS):
        @pl.when(there(-dt, -dc))
        def _(i=i, dt=dt, dc=dc):
            backward(i, dt, dc).wait_recv()

    lane = lax.broadcasted_iota(jnp.int32, (1, 1, LANES), 2)
    sums = [[res_own[t : t + 1, :, b * LANES : (b + 1) * LANES] for b in range(sd // LANES)] for t in range(td)]
    for i, (dt, dc) in enumerate(DIRS):
        start = td - HT if dt < 0 else 0
        for t in range(got[i].shape[0]):
            value = got[i][t : t + 1]
            if dc == 0:
                for b in range(sd // LANES):
                    sums[start + t][b] += value[:, :, b * LANES : (b + 1) * LANES]
            elif dc > 0:
                sums[start + t][0] += jnp.where(lane < HS, value, 0.0)
            else:
                sums[start + t][-1] += jnp.where(lane >= LANES - HS, value, 0.0)
    total = jnp.concatenate([jnp.concatenate(row, axis=2) for row in sums], axis=0)
    for p in range(2):
        scale = F32((sweight.shape[0] if p == 0 else 1) * (hd // td))
        for k in range(covs):
            out_ref[p, k] = total[:, p * covs + k, :] / scale

    for i, (dt, dc) in enumerate(DIRS):
        @pl.when(there(dt, dc))
        def _(i=i, dt=dt, dc=dc):
            forward(i, dt, dc).wait_send()
            backward(i, dt, dc).wait_send()


def body(nt, nc, theta, tangent, covariates, counts, sfirst, sweight, tfirst, tweight):
    covs, sd, td = theta.shape
    cd, hd = counts.shape
    te = td + 2 * HT
    operands = (
        theta.transpose(0, 2, 1), tangent.transpose(0, 2, 1), covariates, counts,
        sfirst.reshape(1, cd), sweight, tfirst.reshape(1, hd), tweight,
    )
    got = [
        pltpu.VMEM((HT if dt else td, SUB, LANES if dc else sd), F32) for dt, dc in DIRS
    ]
    dirs = len(DIRS)
    out = pl.pallas_call(
        functools.partial(kernel, nt, nc),
        out_shape=jax.ShapeDtypeStruct((2, covs, td, sd), F32),
        in_specs=[pl.BlockSpec(memory_space=pltpu.HBM)] * len(operands),
        out_specs=pl.BlockSpec(memory_space=pltpu.VMEM),
        scratch_shapes=[pltpu.VMEM(x.shape, x.dtype) for x in operands]
        + [
            pltpu.VMEM((te, SUB, sd), F32),
            pltpu.VMEM((te, SUB, LANES), F32),
            pltpu.VMEM((te, SUB, LANES), F32),
            pltpu.VMEM((2 * cd, sd + LANES), BF16),
            pltpu.VMEM((4 * te * SUB, hd), BF16),
            pltpu.VMEM((hd, 2 * te * SUB), BF16),
            pltpu.VMEM((2 * te * SUB, cd), BF16),
            pltpu.VMEM((te, SUB, sd), F32),
            pltpu.VMEM((te, SUB, LANES), F32),
            got,
            pltpu.SemaphoreType.DMA((8,)),
            pltpu.SemaphoreType.DMA((dirs,)),
            pltpu.SemaphoreType.DMA((dirs,)),
            pltpu.SemaphoreType.DMA((dirs,)),
            pltpu.SemaphoreType.DMA((dirs,)),
        ],
        compiler_params=pltpu.CompilerParams(
            collective_id=0, has_side_effects=True, vmem_limit_bytes=60 * 1024 * 1024
        ),
        name="hessian_product",
    )(*operands)
    out = out.transpose(0, 1, 3, 2)
    return out[0], out[1]


def solution(mesh):
    return jax.shard_map(
        functools.partial(body, mesh.shape["tm"], mesh.shape["cell"]),
        mesh=mesh,
        in_specs=(
            P(None, "cell", "tm"),
            P(None, "cell", "tm"),
            P(None, "cell", "tm"),
            P("cell", "tm"),
            P("cell"),
            P(None, "cell"),
            P("tm"),
            P(None, "tm"),
        ),
        out_specs=(P(None, "cell", "tm"), P(None, "cell", "tm")),
        check_vma=False,
    )
```

```python
import functools

import jax
import jax.numpy as jnp
from jax import lax
from jax.experimental import pallas as pl
from jax.experimental.pallas import tpu as pltpu
from jax.sharding import PartitionSpec as P

HS = 16
HT = 2
LANES = 128
SUB = 8
CHUNK = 512
MESH = pl.DeviceIdType.MESH
DIRS = [(dt, dc) for dt in (1, -1, 0) for dc in (0, 1, -1) if (dt, dc) != (0, 0)]
F32 = jnp.float32
BF16 = jnp.bfloat16


def split(value):
    head = value.astype(BF16)
    return head, (value - head.astype(F32)).astype(BF16)


def split_wide(value):
    head = value.astype(BF16).astype(F32)
    return head, value - head


def bf16_dot(left, right):
    return lax.dot_general(left, right, (((1,), (0,)), ((), ())), preferred_element_type=F32)


def kernel(
    nt, nc, theta_h, tangent_h, covar_h, counts_h, sfirst_h, sweight_h, tfirst_h, tweight_h, out_ref,
    theta, tangent, covar, counts, sfirst, sweight, tfirst, tweight,
    own, low, high, space, time_rows, time_cols, back,
    res_own, res_edge, got, load_sem, send_sem, recv_sem, back_send, back_recv,
):
    covs, td, sd = theta.shape
    cd, hd = counts.shape
    te = td + 2 * HT
    rows = te * SUB
    me_t, me_c = lax.axis_index("tm"), lax.axis_index("cell")

    loads = [
        pltpu.make_async_copy(src, dst, load_sem.at[i])
        for i, (src, dst) in enumerate(
            [(theta_h, theta), (tangent_h, tangent), (tfirst_h, tfirst), (tweight_h, tweight), (sfirst_h, sfirst), (sweight_h, sweight)]
        )
    ]
    loads[0].start()
    loads[1].start()

    def there(dt, dc):
        inside = me_t >= 0
        if dt:
            inside = jnp.logical_and(inside, (me_t < nt - 1) if dt > 0 else (me_t > 0))
        if dc:
            inside = jnp.logical_and(inside, (me_c < nc - 1) if dc > 0 else (me_c > 0))
        return inside

    def device(dt, dc):
        return {"tm": me_t + dt, "cell": me_c + dc}

    for ref in [own, low, high] + got:
        ref[...] = jnp.zeros(ref.shape, F32)
    barrier = pltpu.get_barrier_semaphore()
    for dt, dc in DIRS:
        @pl.when(there(dt, dc))
        def _(dt=dt, dc=dc):
            pl.semaphore_signal(barrier, inc=1, device_id=device(dt, dc), device_id_type=MESH)

    for copy in loads[2:]:
        copy.start()
    chunk_loads = [
        pltpu.make_async_copy(covar_h, covar, load_sem.at[6]),
        pltpu.make_async_copy(counts_h, counts, load_sem.at[7]),
    ]
    for copy in chunk_loads:
        copy.start()

    loads[0].wait()
    loads[1].wait()
    for p, ref in enumerate((theta, tangent)):
        for k in range(covs):
            own[0:td, p * covs + k, :] = ref[k]

    beside_t = (me_t > 0).astype(jnp.int32) + (me_t < nt - 1).astype(jnp.int32)
    beside_c = (me_c > 0).astype(jnp.int32) + (me_c < nc - 1).astype(jnp.int32)
    pl.semaphore_wait(barrier, (beside_t + 1) * (beside_c + 1) - 1)

    def forward(i, dt, dc):
        src_t = {0: pl.ds(0, td), 1: pl.ds(td - HT, HT), -1: pl.ds(0, HT)}[dt]
        dst_t = {0: pl.ds(0, td), 1: pl.ds(td, HT), -1: pl.ds(td + HT, HT)}[dt]
        src_s = {0: pl.ds(0, sd), 1: pl.ds(sd - LANES, LANES), -1: pl.ds(0, LANES)}[dc]
        dst = {0: own, 1: low, -1: high}[dc]
        return pltpu.make_async_remote_copy(
            src_ref=own.at[src_t, :, src_s], dst_ref=dst.at[dst_t],
            send_sem=send_sem.at[i], recv_sem=recv_sem.at[i], device_id=device(dt, dc), device_id_type=MESH,
        )

    for i, (dt, dc) in enumerate(DIRS):
        @pl.when(there(dt, dc))
        def _(i=i, dt=dt, dc=dc):
            forward(i, dt, dc).start()

    loads[2].wait()
    loads[3].wait()
    index = lax.broadcasted_iota(jnp.int32, (rows, LANES), 0) >> (SUB.bit_length() - 1)
    place = jnp.where(index < td, index, jnp.where(index < td + HT, index - (td + HT), index - HT)) + me_t * td
    diffs = jnp.concatenate([place] * (hd // LANES), axis=1) - tfirst[...]
    basis = jnp.zeros((rows, hd), F32)
    for j in range(tweight.shape[0]):
        basis = jnp.where(diffs == j, tweight[j : j + 1, :], basis)
    head, rest = split_wide(basis)
    turned = jnp.concatenate([head, rest], axis=0).T.astype(BF16)
    time_cols[...] = turned
    head, rest = head.astype(BF16), rest.astype(BF16)
    time_rows[...] = jnp.concatenate([head, head, rest, rest], axis=0)

    loads[4].wait()
    loads[5].wait()
    first = sfirst[...]
    support = sweight.shape[0]
    taps = jnp.concatenate([sweight[...], jnp.zeros((SUB, cd), F32)], axis=0)
    shift = 1
    while shift < SUB:
        taps = jnp.where((first & shift) != 0, pltpu.roll(taps, shift, 0), taps)
        shift *= 2
    group = jnp.broadcast_to((first >> (SUB.bit_length() - 1)) - me_c * (sd // SUB), (SUB, cd))
    blank = jnp.zeros((SUB, cd), F32)
    for block in range(sd // LANES + 1):
        parts = []
        for g in range(LANES // SUB):
            if block < sd // LANES:
                number = block * (LANES // SUB) + g
            elif g < HS // SUB:
                number = sd // SUB + g
            elif g >= (LANES - HS) // SUB:
                number = g - LANES // SUB
            else:
                parts.append(blank)
                continue
            part = blank
            for m in range(support // SUB + 1):
                part = jnp.where(group == number - m, taps[m * SUB : (m + 1) * SUB], part)
            parts.append(part)
        head, rest = split(jnp.concatenate(parts, axis=0).T)
        space[:cd, block * LANES : (block + 1) * LANES] = head
        space[cd:, block * LANES : (block + 1) * LANES] = rest

    for i, (dt, dc) in enumerate(DIRS):
        @pl.when(there(-dt, -dc))
        def _(i=i, dt=dt, dc=dc):
            forward(i, dt, dc).wait_recv()

    lane = lax.broadcasted_iota(jnp.int32, (rows, LANES), 1)
    edge = jnp.where(lane < HS, high[...].reshape(rows, LANES), jnp.where(lane >= LANES - HS, low[...].reshape(rows, LANES), 0.0))
    head, rest = split(jnp.concatenate([own[...].reshape(rows, sd), edge], axis=1))
    coef = jnp.concatenate([head, rest], axis=0)
    nt_dims = (((1,), (1,)), ((), ()))
    value = lax.dot_general(space[...], coef, nt_dims, preferred_element_type=F32)
    value = value[:cd] + value[cd:]
    value = value + pltpu.roll(value, rows, 1)
    head, rest = split_wide(value)
    wide = lax.broadcasted_iota(jnp.int32, (cd, 2 * rows), 1)
    spatial = jnp.where(wide < rows, head, rest)

    for copy in chunk_loads:
        copy.wait()
    lane = lax.broadcasted_iota(jnp.int32, (CHUNK, 2 * rows), 1)
    which = lane & (SUB - 1)
    for start in range(0, cd, CHUNK):
        part = slice(start, start + CHUNK)
        fields = []
        for n in range(2 * covs):
            picked = jnp.where(which == n, spatial[part], 0.0).astype(BF16)
            fields.append(bf16_dot(jnp.concatenate([picked, picked], axis=1), time_rows[...]))
        predictor = covar[0, part, :] * fields[0]
        tangent_pred = covar[0, part, :] * fields[covs]
        for k in range(1, covs):
            predictor = predictor + covar[k, part, :] * fields[k]
            tangent_pred = tangent_pred + covar[k, part, :] * fields[covs + k]
        rates = jnp.exp(predictor)
        factors = (rates * tangent_pred, counts[part, :].astype(F32) - rates)
        total = jnp.zeros((CHUNK, 2 * rows), F32)
        for n in range(2 * covs):
            head, rest = split(covar[n % covs, part, :] * factors[n // covs])
            value = bf16_dot(jnp.concatenate([head, rest], axis=0), time_cols[...])
            total = jnp.where(which == n, value[:CHUNK] + value[CHUNK:], total)
        total = total + pltpu.roll(total, rows, 1)
        head, rest = split_wide(total)
        back[:, part] = jnp.where(lane < rows, head, rest).T.astype(BF16)

    def backward(i, dt, dc):
        src_t = {0: pl.ds(0, td), 1: pl.ds(td + HT, HT), -1: pl.ds(td, HT)}[dt]
        src = res_edge if dc else res_own
        return pltpu.make_async_remote_copy(
            src_ref=src.at[src_t], dst_ref=got[i],
            send_sem=back_send.at[i], recv_sem=back_recv.at[i], device_id=device(dt, dc), device_id_type=MESH,
        )

    for edges in (True, False):
        columns = slice(sd, sd + LANES) if edges else slice(0, sd)
        result = bf16_dot(jnp.concatenate([back[...], back[...]], axis=1), space[:, columns])
        result = result[:rows] + result[rows:]
        (res_edge if edges else res_own)[...] = result.reshape(te, SUB, LANES if edges else sd)
        for i, (dt, dc) in enumerate(DIRS):
            if (dc != 0) == edges:
                @pl.when(there(dt, dc))
                def _(i=i, dt=dt, dc=dc):
                    backward(i, dt, dc).start()
    for i, (dt, dc) in enumerate(DIRS):
        @pl.when(there(-dt, -dc))
        def _(i=i, dt=dt, dc=dc):
            backward(i, dt, dc).wait_recv()

    lane = lax.broadcasted_iota(jnp.int32, (1, 1, LANES), 2)
    sums = [[res_own[t : t + 1, :, b * LANES : (b + 1) * LANES] for b in range(sd // LANES)] for t in range(td)]
    for i, (dt, dc) in enumerate(DIRS):
        start = td - HT if dt < 0 else 0
        for t in range(got[i].shape[0]):
            value = got[i][t : t + 1]
            if dc == 0:
                for b in range(sd // LANES):
                    sums[start + t][b] += value[:, :, b * LANES : (b + 1) * LANES]
            elif dc > 0:
                sums[start + t][0] += jnp.where(lane < HS, value, 0.0)
            else:
                sums[start + t][-1] += jnp.where(lane >= LANES - HS, value, 0.0)
    total = jnp.concatenate([jnp.concatenate(row, axis=2) for row in sums], axis=0)
    for p in range(2):
        scale = F32((sweight.shape[0] if p == 0 else 1) * (hd // td))
        for k in range(covs):
            out_ref[p, k] = total[:, p * covs + k, :] / scale

    for i, (dt, dc) in enumerate(DIRS):
        @pl.when(there(dt, dc))
        def _(i=i, dt=dt, dc=dc):
            forward(i, dt, dc).wait_send()
            backward(i, dt, dc).wait_send()


def body(nt, nc, theta, tangent, covariates, counts, sfirst, sweight, tfirst, tweight):
    covs, sd, td = theta.shape
    cd, hd = counts.shape
    te = td + 2 * HT
    operands = (
        theta.transpose(0, 2, 1), tangent.transpose(0, 2, 1), covariates, counts,
        sfirst.reshape(1, cd), sweight, tfirst.reshape(1, hd), tweight,
    )
    got = [
        pltpu.VMEM((HT if dt else td, SUB, LANES if dc else sd), F32) for dt, dc in DIRS
    ]
    dirs = len(DIRS)
    out = pl.pallas_call(
        functools.partial(kernel, nt, nc),
        out_shape=jax.ShapeDtypeStruct((2, covs, td, sd), F32),
        in_specs=[pl.BlockSpec(memory_space=pltpu.HBM)] * len(operands),
        out_specs=pl.BlockSpec(memory_space=pltpu.VMEM),
        scratch_shapes=[pltpu.VMEM(x.shape, x.dtype) for x in operands]
        + [
            pltpu.VMEM((te, SUB, sd), F32),
            pltpu.VMEM((te, SUB, LANES), F32),
            pltpu.VMEM((te, SUB, LANES), F32),
            pltpu.VMEM((2 * cd, sd + LANES), BF16),
            pltpu.VMEM((4 * te * SUB, hd), BF16),
            pltpu.VMEM((hd, 2 * te * SUB), BF16),
            pltpu.VMEM((2 * te * SUB, cd), BF16),
            pltpu.VMEM((te, SUB, sd), F32),
            pltpu.VMEM((te, SUB, LANES), F32),
            got,
            pltpu.SemaphoreType.DMA((8,)),
            pltpu.SemaphoreType.DMA((dirs,)),
            pltpu.SemaphoreType.DMA((dirs,)),
            pltpu.SemaphoreType.DMA((dirs,)),
            pltpu.SemaphoreType.DMA((dirs,)),
        ],
        compiler_params=pltpu.CompilerParams(
            collective_id=0, has_side_effects=True, vmem_limit_bytes=60 * 1024 * 1024
        ),
        name="hessian_product",
    )(*operands)
    out = out.transpose(0, 1, 3, 2)
    return out[0], out[1]


def solution(mesh):
    return jax.shard_map(
        functools.partial(body, mesh.shape["tm"], mesh.shape["cell"]),
        mesh=mesh,
        in_specs=(
            P(None, "cell", "tm"),
            P(None, "cell", "tm"),
            P(None, "cell", "tm"),
            P("cell", "tm"),
            P("cell"),
            P(None, "cell"),
            P("tm"),
            P(None, "tm"),
        ),
        out_specs=(P(None, "cell", "tm"), P(None, "cell", "tm")),
        check_vma=False,
    )
```

```python
import functools

import jax
import jax.numpy as jnp
from jax import lax
from jax.experimental import pallas as pl
from jax.experimental.pallas import tpu as pltpu
from jax.sharding import PartitionSpec as P

HS = 16
HT = 2
LANES = 128
SUB = 8
CHUNK = 256
MESH = pl.DeviceIdType.MESH
DIRS = [(dt, dc) for dt in (1, -1, 0) for dc in (0, 1, -1) if (dt, dc) != (0, 0)]
F32 = jnp.float32
BF16 = jnp.bfloat16


def split(value):
    head = value.astype(BF16)
    return head, (value - head.astype(F32)).astype(BF16)


def split_wide(value):
    head = value.astype(BF16).astype(F32)
    return head, value - head


def bf16_dot(left, right):
    return lax.dot_general(left, right, (((1,), (0,)), ((), ())), preferred_element_type=F32)


def kernel(
    nt, nc, theta_h, tangent_h, covar_h, counts_h, sfirst_h, sweight_h, tfirst_h, tweight_h, out_ref,
    theta, tangent, covar, counts, sfirst, sweight, tfirst, tweight,
    own, low, high, space, time_rows, time_cols, back,
    res_own, res_edge, got, load_sem, send_sem, recv_sem, back_send, back_recv,
):
    covs, td, sd = theta.shape
    cd, hd = counts.shape
    te = td + 2 * HT
    rows = te * SUB
    me_t, me_c = lax.axis_index("tm"), lax.axis_index("cell")

    loads = [
        pltpu.make_async_copy(src, dst, load_sem.at[i])
        for i, (src, dst) in enumerate(
            [(theta_h, theta), (tangent_h, tangent), (tfirst_h, tfirst), (tweight_h, tweight), (sfirst_h, sfirst), (sweight_h, sweight)]
        )
    ]
    loads[0].start()
    loads[1].start()

    def there(dt, dc):
        inside = me_t >= 0
        if dt:
            inside = jnp.logical_and(inside, (me_t < nt - 1) if dt > 0 else (me_t > 0))
        if dc:
            inside = jnp.logical_and(inside, (me_c < nc - 1) if dc > 0 else (me_c > 0))
        return inside

    def device(dt, dc):
        return {"tm": me_t + dt, "cell": me_c + dc}

    for ref in [own, low, high] + got:
        ref[...] = jnp.zeros(ref.shape, F32)
    barrier = pltpu.get_barrier_semaphore()
    for dt, dc in DIRS:
        @pl.when(there(dt, dc))
        def _(dt=dt, dc=dc):
            pl.semaphore_signal(barrier, inc=1, device_id=device(dt, dc), device_id_type=MESH)

    for copy in loads[2:]:
        copy.start()
    chunk_loads = [
        pltpu.make_async_copy(covar_h, covar, load_sem.at[6]),
        pltpu.make_async_copy(counts_h, counts, load_sem.at[7]),
    ]
    for copy in chunk_loads:
        copy.start()

    loads[0].wait()
    loads[1].wait()
    for p, ref in enumerate((theta, tangent)):
        for k in range(covs):
            own[0:td, p * covs + k, :] = ref[k]

    beside_t = (me_t > 0).astype(jnp.int32) + (me_t < nt - 1).astype(jnp.int32)
    beside_c = (me_c > 0).astype(jnp.int32) + (me_c < nc - 1).astype(jnp.int32)
    pl.semaphore_wait(barrier, (beside_t + 1) * (beside_c + 1) - 1)

    def forward(i, dt, dc):
        src_t = {0: pl.ds(0, td), 1: pl.ds(td - HT, HT), -1: pl.ds(0, HT)}[dt]
        dst_t = {0: pl.ds(0, td), 1: pl.ds(td, HT), -1: pl.ds(td + HT, HT)}[dt]
        src_s = {0: pl.ds(0, sd), 1: pl.ds(sd - LANES, LANES), -1: pl.ds(0, LANES)}[dc]
        dst = {0: own, 1: low, -1: high}[dc]
        return pltpu.make_async_remote_copy(
            src_ref=own.at[src_t, :, src_s], dst_ref=dst.at[dst_t],
            send_sem=send_sem.at[i], recv_sem=recv_sem.at[i], device_id=device(dt, dc), device_id_type=MESH,
        )

    for i, (dt, dc) in enumerate(DIRS):
        @pl.when(there(dt, dc))
        def _(i=i, dt=dt, dc=dc):
            forward(i, dt, dc).start()

    loads[2].wait()
    loads[3].wait()
    index = lax.broadcasted_iota(jnp.int32, (rows, LANES), 0) >> (SUB.bit_length() - 1)
    place = jnp.where(index < td, index, jnp.where(index < td + HT, index - (td + HT), index - HT)) + me_t * td
    diffs = jnp.concatenate([place] * (hd // LANES), axis=1) - tfirst[...]
    basis = jnp.zeros((rows, hd), F32)
    for j in range(tweight.shape[0]):
        basis = jnp.where(diffs == j, tweight[j : j + 1, :], basis)
    head, rest = split_wide(basis)
    turned = jnp.concatenate([head, rest], axis=0).T.astype(BF16)
    time_cols[...] = turned
    head, rest = head.astype(BF16), rest.astype(BF16)
    time_rows[...] = jnp.concatenate([head, head, rest, rest], axis=0)

    loads[4].wait()
    loads[5].wait()
    first = sfirst[...]
    support = sweight.shape[0]
    taps = jnp.concatenate([sweight[...], jnp.zeros((SUB, cd), F32)], axis=0)
    shift = 1
    while shift < SUB:
        taps = jnp.where((first & shift) != 0, pltpu.roll(taps, shift, 0), taps)
        shift *= 2
    group = jnp.broadcast_to((first >> (SUB.bit_length() - 1)) - me_c * (sd // SUB), (SUB, cd))
    blank = jnp.zeros((SUB, cd), F32)
    for block in range(sd // LANES + 1):
        parts = []
        for g in range(LANES // SUB):
            if block < sd // LANES:
                number = block * (LANES // SUB) + g
            elif g < HS // SUB:
                number = sd // SUB + g
            elif g >= (LANES - HS) // SUB:
                number = g - LANES // SUB
            else:
                parts.append(blank)
                continue
            part = blank
            for m in range(support // SUB + 1):
                part = jnp.where(group == number - m, taps[m * SUB : (m + 1) * SUB], part)
            parts.append(part)
        head, rest = split(jnp.concatenate(parts, axis=0).T)
        space[:cd, block * LANES : (block + 1) * LANES] = head
        space[cd:, block * LANES : (block + 1) * LANES] = rest

    for i, (dt, dc) in enumerate(DIRS):
        @pl.when(there(-dt, -dc))
        def _(i=i, dt=dt, dc=dc):
            forward(i, dt, dc).wait_recv()

    lane = lax.broadcasted_iota(jnp.int32, (rows, LANES), 1)
    edge = jnp.where(lane < HS, high[...].reshape(rows, LANES), jnp.where(lane >= LANES - HS, low[...].reshape(rows, LANES), 0.0))
    head, rest = split(jnp.concatenate([own[...].reshape(rows, sd), edge], axis=1))
    coef = jnp.concatenate([head, rest], axis=0)
    nt_dims = (((1,), (1,)), ((), ()))
    value = lax.dot_general(space[...], coef, nt_dims, preferred_element_type=F32)
    value = value[:cd] + value[cd:]
    value = value + pltpu.roll(value, rows, 1)
    head, rest = split_wide(value)
    wide = lax.broadcasted_iota(jnp.int32, (cd, 2 * rows), 1)
    spatial = jnp.where(wide < rows, head, rest)

    for copy in chunk_loads:
        copy.wait()
    lane = lax.broadcasted_iota(jnp.int32, (cd, 2 * rows), 1)
    which = lane & (SUB - 1)
    picked = []
    for n in range(2 * covs):
        value = jnp.where(which == n, spatial, 0.0).astype(BF16)
        picked.append(jnp.concatenate([value, value], axis=1))
    total = jnp.zeros((cd, 2 * rows), F32)
    for start in range(0, hd, CHUNK):
        part = slice(start, start + CHUNK)
        fields = [bf16_dot(value, time_rows[:, part]) for value in picked]
        predictor = covar[0, :, part] * fields[0]
        tangent_pred = covar[0, :, part] * fields[covs]
        for k in range(1, covs):
            predictor = predictor + covar[k, :, part] * fields[k]
            tangent_pred = tangent_pred + covar[k, :, part] * fields[covs + k]
        rates = jnp.exp(predictor)
        factors = (rates * tangent_pred, counts[:, part].astype(F32) - rates)
        sums = jnp.zeros((cd, 2 * rows), F32)
        for n in range(2 * covs):
            head, rest = split(covar[n % covs, :, part] * factors[n // covs])
            value = bf16_dot(jnp.concatenate([head, rest], axis=0), time_cols[part])
            sums = jnp.where(which == n, value[:cd] + value[cd:], sums)
        total = total + sums
    total = total + pltpu.roll(total, rows, 1)
    head, rest = split_wide(total)
    back[...] = jnp.where(lane < rows, head, rest).T.astype(BF16)

    def backward(i, dt, dc):
        src_t = {0: pl.ds(0, td), 1: pl.ds(td + HT, HT), -1: pl.ds(td, HT)}[dt]
        src = res_edge if dc else res_own
        return pltpu.make_async_remote_copy(
            src_ref=src.at[src_t], dst_ref=got[i],
            send_sem=back_send.at[i], recv_sem=back_recv.at[i], device_id=device(dt, dc), device_id_type=MESH,
        )

    for edges in (True, False):
        columns = slice(sd, sd + LANES) if edges else slice(0, sd)
        result = bf16_dot(jnp.concatenate([back[...], back[...]], axis=1), space[:, columns])
        result = result[:rows] + result[rows:]
        (res_edge if edges else res_own)[...] = result.reshape(te, SUB, LANES if edges else sd)
        for i, (dt, dc) in enumerate(DIRS):
            if (dc != 0) == edges:
                @pl.when(there(dt, dc))
                def _(i=i, dt=dt, dc=dc):
                    backward(i, dt, dc).start()
    for i, (dt, dc) in enumerate(DIRS):
        @pl.when(there(-dt, -dc))
        def _(i=i, dt=dt, dc=dc):
            backward(i, dt, dc).wait_recv()

    lane = lax.broadcasted_iota(jnp.int32, (1, 1, LANES), 2)
    sums = [[res_own[t : t + 1, :, b * LANES : (b + 1) * LANES] for b in range(sd // LANES)] for t in range(td)]
    for i, (dt, dc) in enumerate(DIRS):
        start = td - HT if dt < 0 else 0
        for t in range(got[i].shape[0]):
            value = got[i][t : t + 1]
            if dc == 0:
                for b in range(sd // LANES):
                    sums[start + t][b] += value[:, :, b * LANES : (b + 1) * LANES]
            elif dc > 0:
                sums[start + t][0] += jnp.where(lane < HS, value, 0.0)
            else:
                sums[start + t][-1] += jnp.where(lane >= LANES - HS, value, 0.0)
    total = jnp.concatenate([jnp.concatenate(row, axis=2) for row in sums], axis=0)
    for p in range(2):
        scale = F32((sweight.shape[0] if p == 0 else 1) * (hd // td))
        for k in range(covs):
            out_ref[p, k] = total[:, p * covs + k, :] / scale

    for i, (dt, dc) in enumerate(DIRS):
        @pl.when(there(dt, dc))
        def _(i=i, dt=dt, dc=dc):
            forward(i, dt, dc).wait_send()
            backward(i, dt, dc).wait_send()


def body(nt, nc, theta, tangent, covariates, counts, sfirst, sweight, tfirst, tweight):
    covs, sd, td = theta.shape
    cd, hd = counts.shape
    te = td + 2 * HT
    operands = (
        theta.transpose(0, 2, 1), tangent.transpose(0, 2, 1), covariates, counts,
        sfirst.reshape(1, cd), sweight, tfirst.reshape(1, hd), tweight,
    )
    got = [
        pltpu.VMEM((HT if dt else td, SUB, LANES if dc else sd), F32) for dt, dc in DIRS
    ]
    dirs = len(DIRS)
    out = pl.pallas_call(
        functools.partial(kernel, nt, nc),
        out_shape=jax.ShapeDtypeStruct((2, covs, td, sd), F32),
        in_specs=[pl.BlockSpec(memory_space=pltpu.HBM)] * len(operands),
        out_specs=pl.BlockSpec(memory_space=pltpu.VMEM),
        scratch_shapes=[pltpu.VMEM(x.shape, x.dtype) for x in operands]
        + [
            pltpu.VMEM((te, SUB, sd), F32),
            pltpu.VMEM((te, SUB, LANES), F32),
            pltpu.VMEM((te, SUB, LANES), F32),
            pltpu.VMEM((2 * cd, sd + LANES), BF16),
            pltpu.VMEM((4 * te * SUB, hd), BF16),
            pltpu.VMEM((hd, 2 * te * SUB), BF16),
            pltpu.VMEM((2 * te * SUB, cd), BF16),
            pltpu.VMEM((te, SUB, sd), F32),
            pltpu.VMEM((te, SUB, LANES), F32),
            got,
            pltpu.SemaphoreType.DMA((8,)),
            pltpu.SemaphoreType.DMA((dirs,)),
            pltpu.SemaphoreType.DMA((dirs,)),
            pltpu.SemaphoreType.DMA((dirs,)),
            pltpu.SemaphoreType.DMA((dirs,)),
        ],
        compiler_params=pltpu.CompilerParams(
            collective_id=0, has_side_effects=True, vmem_limit_bytes=60 * 1024 * 1024
        ),
        name="hessian_product",
    )(*operands)
    out = out.transpose(0, 1, 3, 2)
    return out[0], out[1]


def solution(mesh):
    return jax.shard_map(
        functools.partial(body, mesh.shape["tm"], mesh.shape["cell"]),
        mesh=mesh,
        in_specs=(
            P(None, "cell", "tm"),
            P(None, "cell", "tm"),
            P(None, "cell", "tm"),
            P("cell", "tm"),
            P("cell"),
            P(None, "cell"),
            P("tm"),
            P(None, "tm"),
        ),
        out_specs=(P(None, "cell", "tm"), P(None, "cell", "tm")),
        check_vma=False,
    )
```

```python
import functools

import jax
import jax.numpy as jnp
from jax import lax
from jax.experimental import pallas as pl
from jax.experimental.pallas import tpu as pltpu
from jax.sharding import PartitionSpec as P

HS = 16
HT = 2
LANES = 128
SUB = 8
CHUNK = 256
MESH = pl.DeviceIdType.MESH
DIRS = [(1, 1), (1, -1), (-1, 1), (-1, -1), (0, 1), (0, -1), (1, 0), (-1, 0)]
F32 = jnp.float32
BF16 = jnp.bfloat16


def split(value):
    head = value.astype(BF16)
    return head, (value - head.astype(F32)).astype(BF16)


def split_wide(value):
    head = value.astype(BF16).astype(F32)
    return head, value - head


def bf16_dot(left, right):
    return lax.dot_general(left, right, (((1,), (0,)), ((), ())), preferred_element_type=F32)


def kernel(
    nt, nc, theta_h, tangent_h, covar_h, counts_h, sfirst_h, sweight_h, tfirst_h, tweight_h, hess_ref, grad_ref,
    theta, tangent, covar, counts, sfirst, sweight, tfirst, tweight,
    own, low, high, space, time_rows, time_cols, back,
    res_own, res_edge, got, load_sem, send_sem, recv_sem, back_send, back_recv,
):
    covs, td, sd = theta.shape
    cd, hd = counts.shape
    te = td + 2 * HT
    rows = te * SUB
    me_t, me_c = lax.axis_index("tm"), lax.axis_index("cell")

    loads = [
        pltpu.make_async_copy(src, dst, load_sem.at[i])
        for i, (src, dst) in enumerate(
            [(theta_h, theta), (tangent_h, tangent), (tfirst_h, tfirst), (tweight_h, tweight), (sfirst_h, sfirst), (sweight_h, sweight)]
        )
    ]
    loads[0].start()
    loads[1].start()

    def there(dt, dc):
        inside = me_t >= 0
        if dt:
            inside = jnp.logical_and(inside, (me_t < nt - 1) if dt > 0 else (me_t > 0))
        if dc:
            inside = jnp.logical_and(inside, (me_c < nc - 1) if dc > 0 else (me_c > 0))
        return inside

    def device(dt, dc):
        return {"tm": me_t + dt, "cell": me_c + dc}

    for ref in [own, low, high] + got:
        ref[...] = jnp.zeros(ref.shape, F32)
    barrier = pltpu.get_barrier_semaphore()
    for dt, dc in DIRS:
        @pl.when(there(dt, dc))
        def _(dt=dt, dc=dc):
            pl.semaphore_signal(barrier, inc=1, device_id=device(dt, dc), device_id_type=MESH)

    for copy in loads[2:]:
        copy.start()
    chunk_loads = [
        pltpu.make_async_copy(covar_h, covar, load_sem.at[6]),
        pltpu.make_async_copy(counts_h, counts, load_sem.at[7]),
    ]
    for copy in chunk_loads:
        copy.start()

    loads[0].wait()
    loads[1].wait()
    for p, ref in enumerate((theta, tangent)):
        for k in range(covs):
            own[0:td, p * covs + k, :] = ref[k]

    beside_t = (me_t > 0).astype(jnp.int32) + (me_t < nt - 1).astype(jnp.int32)
    beside_c = (me_c > 0).astype(jnp.int32) + (me_c < nc - 1).astype(jnp.int32)
    pl.semaphore_wait(barrier, (beside_t + 1) * (beside_c + 1) - 1)

    def forward(i, dt, dc):
        src_t = {0: pl.ds(0, td), 1: pl.ds(td - HT, HT), -1: pl.ds(0, HT)}[dt]
        dst_t = {0: pl.ds(0, td), 1: pl.ds(td, HT), -1: pl.ds(td + HT, HT)}[dt]
        src_s = {0: pl.ds(0, sd), 1: pl.ds(sd - LANES, LANES), -1: pl.ds(0, LANES)}[dc]
        dst = {0: own, 1: low, -1: high}[dc]
        return pltpu.make_async_remote_copy(
            src_ref=own.at[src_t, :, src_s], dst_ref=dst.at[dst_t],
            send_sem=send_sem.at[i], recv_sem=recv_sem.at[i], device_id=device(dt, dc), device_id_type=MESH,
        )

    for i, (dt, dc) in enumerate(DIRS):
        @pl.when(there(dt, dc))
        def _(i=i, dt=dt, dc=dc):
            forward(i, dt, dc).start()

    loads[2].wait()
    loads[3].wait()
    index = lax.broadcasted_iota(jnp.int32, (rows, LANES), 0) >> (SUB.bit_length() - 1)
    place = jnp.where(index < td, index, jnp.where(index < td + HT, index - (td + HT), index - HT)) + me_t * td
    diffs = jnp.concatenate([place] * (hd // LANES), axis=1) - tfirst[...]
    basis = jnp.zeros((rows, hd), F32)
    for j in range(tweight.shape[0]):
        basis = jnp.where(diffs == j, tweight[j : j + 1, :], basis)
    head, rest = split_wide(basis)
    turned = jnp.concatenate([head, rest], axis=0).T.astype(BF16)
    time_cols[...] = turned
    head, rest = head.astype(BF16), rest.astype(BF16)
    time_rows[...] = jnp.concatenate([head, head, rest, rest], axis=0)

    loads[4].wait()
    loads[5].wait()
    first = sfirst[...]
    support = sweight.shape[0]
    taps = jnp.concatenate([sweight[...], jnp.zeros((SUB, cd), F32)], axis=0)
    shift = 1
    while shift < SUB:
        taps = jnp.where((first & shift) != 0, pltpu.roll(taps, shift, 0), taps)
        shift *= 2
    group = jnp.broadcast_to((first >> (SUB.bit_length() - 1)) - me_c * (sd // SUB), (SUB, cd))
    blank = jnp.zeros((SUB, cd), F32)
    for block in range(sd // LANES + 1):
        parts = []
        for g in range(LANES // SUB):
            if block < sd // LANES:
                number = block * (LANES // SUB) + g
            elif g < HS // SUB:
                number = sd // SUB + g
            elif g >= (LANES - HS) // SUB:
                number = g - LANES // SUB
            else:
                parts.append(blank)
                continue
            part = blank
            for m in range(support // SUB + 1):
                part = jnp.where(group == number - m, taps[m * SUB : (m + 1) * SUB], part)
            parts.append(part)
        head, rest = split(jnp.concatenate(parts, axis=0).T)
        space[:cd, block * LANES : (block + 1) * LANES] = head
        space[cd:, block * LANES : (block + 1) * LANES] = rest

    for i, (dt, dc) in enumerate(DIRS):
        @pl.when(there(-dt, -dc))
        def _(i=i, dt=dt, dc=dc):
            forward(i, dt, dc).wait_recv()

    lane = lax.broadcasted_iota(jnp.int32, (rows, LANES), 1)
    edge = jnp.where(lane < HS, high[...].reshape(rows, LANES), jnp.where(lane >= LANES - HS, low[...].reshape(rows, LANES), 0.0))
    head, rest = split(jnp.concatenate([own[...].reshape(rows, sd), edge], axis=1))
    coef = jnp.concatenate([head, rest], axis=0)
    nt_dims = (((1,), (1,)), ((), ()))
    value = lax.dot_general(space[...], coef, nt_dims, preferred_element_type=F32)
    value = value[:cd] + value[cd:]
    value = value + pltpu.roll(value, rows, 1)
    head, rest = split_wide(value)
    wide = lax.broadcasted_iota(jnp.int32, (cd, 2 * rows), 1)
    spatial = jnp.where(wide < rows, head, rest)

    for copy in chunk_loads:
        copy.wait()
    lane = lax.broadcasted_iota(jnp.int32, (cd, 2 * rows), 1)
    which = lane & (SUB - 1)
    picked = []
    for n in range(2 * covs):
        value = jnp.where(which == n, spatial, 0.0).astype(BF16)
        picked.append(jnp.concatenate([value, value], axis=1))
    total = jnp.zeros((cd, 2 * rows), F32)
    for start in range(0, hd, CHUNK):
        part = slice(start, start + CHUNK)
        fields = [bf16_dot(value, time_rows[:, part]) for value in picked]
        predictor = covar[0, :, part] * fields[0]
        tangent_pred = covar[0, :, part] * fields[covs]
        for k in range(1, covs):
            predictor = predictor + covar[k, :, part] * fields[k]
            tangent_pred = tangent_pred + covar[k, :, part] * fields[covs + k]
        rates = jnp.exp(predictor)
        factors = (rates * tangent_pred, counts[:, part].astype(F32) - rates)
        sums = jnp.zeros((cd, 2 * rows), F32)
        for n in range(2 * covs):
            head, rest = split(covar[n % covs, :, part] * factors[n // covs])
            value = bf16_dot(jnp.concatenate([head, rest], axis=0), time_cols[part])
            sums = jnp.where(which == n, value[:cd] + value[cd:], sums)
        total = total + sums
    total = total + pltpu.roll(total, rows, 1)
    head, rest = split_wide(total)
    back[...] = jnp.where(lane < rows, head, rest).T.astype(BF16)

    def backward(i, dt, dc):
        src_t = {0: pl.ds(0, td), 1: pl.ds(td + HT, HT), -1: pl.ds(td, HT)}[dt]
        src = res_edge if dc else res_own
        return pltpu.make_async_remote_copy(
            src_ref=src.at[src_t], dst_ref=got[i],
            send_sem=back_send.at[i], recv_sem=back_recv.at[i], device_id=device(dt, dc), device_id_type=MESH,
        )

    for edges in (True, False):
        columns = slice(sd, sd + LANES) if edges else slice(0, sd)
        result = bf16_dot(jnp.concatenate([back[...], back[...]], axis=1), space[:, columns])
        result = result[:rows] + result[rows:]
        (res_edge if edges else res_own)[...] = result.reshape(te, SUB, LANES if edges else sd)
        for i, (dt, dc) in enumerate(DIRS):
            if (dc != 0) == edges:
                @pl.when(there(dt, dc))
                def _(i=i, dt=dt, dc=dc):
                    backward(i, dt, dc).start()
    for i, (dt, dc) in enumerate(DIRS):
        @pl.when(there(-dt, -dc))
        def _(i=i, dt=dt, dc=dc):
            backward(i, dt, dc).wait_recv()

    lane = lax.broadcasted_iota(jnp.int32, (1, 1, LANES), 2)
    sums = [[res_own[t : t + 1, :, b * LANES : (b + 1) * LANES] for b in range(sd // LANES)] for t in range(td)]
    for i, (dt, dc) in enumerate(DIRS):
        start = td - HT if dt < 0 else 0
        for t in range(got[i].shape[0]):
            value = got[i][t : t + 1]
            if dc == 0:
                for b in range(sd // LANES):
                    sums[start + t][b] += value[:, :, b * LANES : (b + 1) * LANES]
            elif dc > 0:
                sums[start + t][0] += jnp.where(lane < HS, value, 0.0)
            else:
                sums[start + t][-1] += jnp.where(lane >= LANES - HS, value, 0.0)
    total = jnp.concatenate([jnp.concatenate(row, axis=2) for row in sums], axis=0)
    for p in range(2):
        scale = F32((sweight.shape[0] if p == 0 else 1) * (hd // td))
        for k in range(covs):
            (grad_ref if p else hess_ref)[k] = total[:, p * covs + k, :] / scale

    for i, (dt, dc) in enumerate(DIRS):
        @pl.when(there(dt, dc))
        def _(i=i, dt=dt, dc=dc):
            forward(i, dt, dc).wait_send()
            backward(i, dt, dc).wait_send()


def body(nt, nc, theta, tangent, covariates, counts, sfirst, sweight, tfirst, tweight):
    covs, sd, td = theta.shape
    cd, hd = counts.shape
    te = td + 2 * HT
    operands = (
        theta.transpose(0, 2, 1), tangent.transpose(0, 2, 1), covariates, counts,
        sfirst.reshape(1, cd), sweight, tfirst.reshape(1, hd), tweight,
    )
    got = [
        pltpu.VMEM((HT if dt else td, SUB, LANES if dc else sd), F32) for dt, dc in DIRS
    ]
    dirs = len(DIRS)
    out = pl.pallas_call(
        functools.partial(kernel, nt, nc),
        out_shape=[jax.ShapeDtypeStruct((covs, td, sd), F32)] * 2,
        in_specs=[pl.BlockSpec(memory_space=pltpu.HBM)] * len(operands),
        out_specs=[pl.BlockSpec(memory_space=pltpu.VMEM)] * 2,
        scratch_shapes=[pltpu.VMEM(x.shape, x.dtype) for x in operands]
        + [
            pltpu.VMEM((te, SUB, sd), F32),
            pltpu.VMEM((te, SUB, LANES), F32),
            pltpu.VMEM((te, SUB, LANES), F32),
            pltpu.VMEM((2 * cd, sd + LANES), BF16),
            pltpu.VMEM((4 * te * SUB, hd), BF16),
            pltpu.VMEM((hd, 2 * te * SUB), BF16),
            pltpu.VMEM((2 * te * SUB, cd), BF16),
            pltpu.VMEM((te, SUB, sd), F32),
            pltpu.VMEM((te, SUB, LANES), F32),
            got,
            pltpu.SemaphoreType.DMA((8,)),
            pltpu.SemaphoreType.DMA((dirs,)),
            pltpu.SemaphoreType.DMA((dirs,)),
            pltpu.SemaphoreType.DMA((dirs,)),
            pltpu.SemaphoreType.DMA((dirs,)),
        ],
        compiler_params=pltpu.CompilerParams(
            collective_id=0, has_side_effects=True, vmem_limit_bytes=60 * 1024 * 1024
        ),
        name="hessian_product",
    )(*operands)
    return tuple(value.transpose(0, 2, 1) for value in out)


def solution(mesh):
    return jax.shard_map(
        functools.partial(body, mesh.shape["tm"], mesh.shape["cell"]),
        mesh=mesh,
        in_specs=(
            P(None, "cell", "tm"),
            P(None, "cell", "tm"),
            P(None, "cell", "tm"),
            P("cell", "tm"),
            P("cell"),
            P(None, "cell"),
            P("tm"),
            P(None, "tm"),
        ),
        out_specs=(P(None, "cell", "tm"), P(None, "cell", "tm")),
        check_vma=False,
    )
```

```python
import functools

import jax
import jax.numpy as jnp
from jax import lax
from jax.experimental import pallas as pl
from jax.experimental.pallas import tpu as pltpu
from jax.sharding import PartitionSpec as P

HS = 16
HT = 2
LANES = 128
SUB = 8
CHUNK = 256
MESH = pl.DeviceIdType.MESH
DIRS = [(1, 1), (1, -1), (-1, 1), (-1, -1), (0, 1), (0, -1), (1, 0), (-1, 0)]
F32 = jnp.float32
BF16 = jnp.bfloat16


def split(value):
    head = value.astype(BF16)
    return head, (value - head.astype(F32)).astype(BF16)


def split_wide(value):
    head = value.astype(BF16).astype(F32)
    return head, value - head


def bf16_dot(left, right):
    return lax.dot_general(left, right, (((1,), (0,)), ((), ())), preferred_element_type=F32)


def kernel(
    nt, nc, theta_h, tangent_h, covar_h, counts_h, sfirst_h, sweight_h, tfirst_h, tweight_h, out_ref,
    theta, tangent, covar, counts, sfirst, sweight, tfirst, tweight,
    own, low, high, space, time_rows, time_cols, back,
    res_own, res_edge, got, load_sem, send_sem, recv_sem, back_send, back_recv,
):
    covs, td, sd = theta.shape
    cd, hd = counts.shape
    te = td + 2 * HT
    rows = te * SUB
    me_t, me_c = lax.axis_index("tm"), lax.axis_index("cell")

    loads = [
        pltpu.make_async_copy(src, dst, load_sem.at[i])
        for i, (src, dst) in enumerate(
            [(theta_h, theta), (tangent_h, tangent), (tfirst_h, tfirst), (tweight_h, tweight), (sfirst_h, sfirst), (sweight_h, sweight)]
        )
    ]
    loads[0].start()
    loads[1].start()

    def there(dt, dc):
        inside = me_t >= 0
        if dt:
            inside = jnp.logical_and(inside, (me_t < nt - 1) if dt > 0 else (me_t > 0))
        if dc:
            inside = jnp.logical_and(inside, (me_c < nc - 1) if dc > 0 else (me_c > 0))
        return inside

    def device(dt, dc):
        return {"tm": me_t + dt, "cell": me_c + dc}

    for ref in [own, low, high] + got:
        ref[...] = jnp.zeros(ref.shape, F32)
    barrier = pltpu.get_barrier_semaphore()
    for dt, dc in DIRS:
        @pl.when(there(dt, dc))
        def _(dt=dt, dc=dc):
            pl.semaphore_signal(barrier, inc=1, device_id=device(dt, dc), device_id_type=MESH)

    for copy in loads[2:]:
        copy.start()
    chunk_loads = [
        pltpu.make_async_copy(covar_h, covar, load_sem.at[6]),
        pltpu.make_async_copy(counts_h, counts, load_sem.at[7]),
    ]
    loads[0].wait()
    loads[1].wait()
    for p, ref in enumerate((theta, tangent)):
        for k in range(covs):
            own[0:td, p * covs + k, :] = ref[k]

    beside_t = (me_t > 0).astype(jnp.int32) + (me_t < nt - 1).astype(jnp.int32)
    beside_c = (me_c > 0).astype(jnp.int32) + (me_c < nc - 1).astype(jnp.int32)
    pl.semaphore_wait(barrier, (beside_t + 1) * (beside_c + 1) - 1)

    def forward(i, dt, dc):
        src_t = {0: pl.ds(0, td), 1: pl.ds(td - HT, HT), -1: pl.ds(0, HT)}[dt]
        dst_t = {0: pl.ds(0, td), 1: pl.ds(td, HT), -1: pl.ds(td + HT, HT)}[dt]
        src_s = {0: pl.ds(0, sd), 1: pl.ds(sd - LANES, LANES), -1: pl.ds(0, LANES)}[dc]
        dst = {0: own, 1: low, -1: high}[dc]
        return pltpu.make_async_remote_copy(
            src_ref=own.at[src_t, :, src_s], dst_ref=dst.at[dst_t],
            send_sem=send_sem.at[i], recv_sem=recv_sem.at[i], device_id=device(dt, dc), device_id_type=MESH,
        )

    for i, (dt, dc) in enumerate(DIRS):
        @pl.when(there(dt, dc))
        def _(i=i, dt=dt, dc=dc):
            forward(i, dt, dc).start()

    for copy in chunk_loads:
        copy.start()

    loads[2].wait()
    loads[3].wait()
    index = lax.broadcasted_iota(jnp.int32, (rows, LANES), 0) >> (SUB.bit_length() - 1)
    place = jnp.where(index < td, index, jnp.where(index < td + HT, index - (td + HT), index - HT)) + me_t * td
    diffs = jnp.concatenate([place] * (hd // LANES), axis=1) - tfirst[...]
    basis = jnp.zeros((rows, hd), F32)
    for j in range(tweight.shape[0]):
        basis = jnp.where(diffs == j, tweight[j : j + 1, :], basis)
    head, rest = split_wide(basis)
    turned = jnp.concatenate([head, rest], axis=0).T.astype(BF16)
    time_cols[...] = turned
    head, rest = head.astype(BF16), rest.astype(BF16)
    time_rows[...] = jnp.concatenate([head, head, rest, rest], axis=0)

    loads[4].wait()
    loads[5].wait()
    first = sfirst[...]
    support = sweight.shape[0]
    taps = jnp.concatenate([sweight[...], jnp.zeros((SUB, cd), F32)], axis=0)
    shift = 1
    while shift < SUB:
        taps = jnp.where((first & shift) != 0, pltpu.roll(taps, shift, 0), taps)
        shift *= 2
    group = jnp.broadcast_to((first >> (SUB.bit_length() - 1)) - me_c * (sd // SUB), (SUB, cd))
    blank = jnp.zeros((SUB, cd), F32)
    for block in range(sd // LANES + 1):
        parts = []
        for g in range(LANES // SUB):
            if block < sd // LANES:
                number = block * (LANES // SUB) + g
            elif g < HS // SUB:
                number = sd // SUB + g
            elif g >= (LANES - HS) // SUB:
                number = g - LANES // SUB
            else:
                parts.append(blank)
                continue
            part = blank
            for m in range(support // SUB + 1):
                part = jnp.where(group == number - m, taps[m * SUB : (m + 1) * SUB], part)
            parts.append(part)
        head, rest = split(jnp.concatenate(parts, axis=0).T)
        space[:cd, block * LANES : (block + 1) * LANES] = head
        space[cd:, block * LANES : (block + 1) * LANES] = rest

    for i, (dt, dc) in enumerate(DIRS):
        @pl.when(there(-dt, -dc))
        def _(i=i, dt=dt, dc=dc):
            forward(i, dt, dc).wait_recv()

    lane = lax.broadcasted_iota(jnp.int32, (rows, LANES), 1)
    edge = jnp.where(lane < HS, high[...].reshape(rows, LANES), jnp.where(lane >= LANES - HS, low[...].reshape(rows, LANES), 0.0))
    head, rest = split(jnp.concatenate([own[...].reshape(rows, sd), edge], axis=1))
    coef = jnp.concatenate([head, rest], axis=0)
    nt_dims = (((1,), (1,)), ((), ()))
    value = lax.dot_general(space[...], coef, nt_dims, preferred_element_type=F32)
    value = value[:cd] + value[cd:]
    value = value + pltpu.roll(value, rows, 1)
    head, rest = split_wide(value)
    wide = lax.broadcasted_iota(jnp.int32, (cd, 2 * rows), 1)
    spatial = jnp.where(wide < rows, head, rest)

    for copy in chunk_loads:
        copy.wait()
    lane = lax.broadcasted_iota(jnp.int32, (cd, 2 * rows), 1)
    which = lane & (SUB - 1)
    picked = []
    for n in range(2 * covs):
        value = jnp.where(which == n, spatial, 0.0).astype(BF16)
        picked.append(jnp.concatenate([value, value], axis=1))
    total = jnp.zeros((cd, 2 * rows), F32)
    for start in range(0, hd, CHUNK):
        part = slice(start, start + CHUNK)
        fields = [bf16_dot(value, time_rows[:, part]) for value in picked]
        predictor = covar[0, :, part] * fields[0]
        tangent_pred = covar[0, :, part] * fields[covs]
        for k in range(1, covs):
            predictor = predictor + covar[k, :, part] * fields[k]
            tangent_pred = tangent_pred + covar[k, :, part] * fields[covs + k]
        rates = jnp.exp(predictor)
        factors = (rates * tangent_pred, counts[:, part].astype(F32) - rates)
        sums = jnp.zeros((cd, 2 * rows), F32)
        for n in range(2 * covs):
            head, rest = split(covar[n % covs, :, part] * factors[n // covs])
            value = bf16_dot(jnp.concatenate([head, rest], axis=0), time_cols[part])
            sums = jnp.where(which == n, value[:cd] + value[cd:], sums)
        total = total + sums
    total = total + pltpu.roll(total, rows, 1)
    head, rest = split_wide(total)
    back[...] = jnp.where(lane < rows, head, rest).T.astype(BF16)

    def backward(i, dt, dc):
        src_t = {0: pl.ds(0, td), 1: pl.ds(td + HT, HT), -1: pl.ds(td, HT)}[dt]
        src = res_edge if dc else res_own
        return pltpu.make_async_remote_copy(
            src_ref=src.at[src_t], dst_ref=got[i],
            send_sem=back_send.at[i], recv_sem=back_recv.at[i], device_id=device(dt, dc), device_id_type=MESH,
        )

    for edges in (True, False):
        columns = slice(sd, sd + LANES) if edges else slice(0, sd)
        result = bf16_dot(jnp.concatenate([back[...], back[...]], axis=1), space[:, columns])
        result = result[:rows] + result[rows:]
        (res_edge if edges else res_own)[...] = result.reshape(te, SUB, LANES if edges else sd)
        for i, (dt, dc) in enumerate(DIRS):
            if (dc != 0) == edges:
                @pl.when(there(dt, dc))
                def _(i=i, dt=dt, dc=dc):
                    backward(i, dt, dc).start()
    for i, (dt, dc) in enumerate(DIRS):
        @pl.when(there(-dt, -dc))
        def _(i=i, dt=dt, dc=dc):
            backward(i, dt, dc).wait_recv()

    lane = lax.broadcasted_iota(jnp.int32, (1, 1, LANES), 2)
    sums = [[res_own[t : t + 1, :, b * LANES : (b + 1) * LANES] for b in range(sd // LANES)] for t in range(td)]
    for i, (dt, dc) in enumerate(DIRS):
        start = td - HT if dt < 0 else 0
        for t in range(got[i].shape[0]):
            value = got[i][t : t + 1]
            if dc == 0:
                for b in range(sd // LANES):
                    sums[start + t][b] += value[:, :, b * LANES : (b + 1) * LANES]
            elif dc > 0:
                sums[start + t][0] += jnp.where(lane < HS, value, 0.0)
            else:
                sums[start + t][-1] += jnp.where(lane >= LANES - HS, value, 0.0)
    total = jnp.concatenate([jnp.concatenate(row, axis=2) for row in sums], axis=0)
    for p in range(2):
        scale = F32((sweight.shape[0] if p == 0 else 1) * (hd // td))
        for k in range(covs):
            out_ref[p, k] = total[:, p * covs + k, :] / scale

    for i, (dt, dc) in enumerate(DIRS):
        @pl.when(there(dt, dc))
        def _(i=i, dt=dt, dc=dc):
            forward(i, dt, dc).wait_send()
            backward(i, dt, dc).wait_send()


def body(nt, nc, theta, tangent, covariates, counts, sfirst, sweight, tfirst, tweight):
    covs, sd, td = theta.shape
    cd, hd = counts.shape
    te = td + 2 * HT
    operands = (
        theta.transpose(0, 2, 1), tangent.transpose(0, 2, 1), covariates, counts,
        sfirst.reshape(1, cd), sweight, tfirst.reshape(1, hd), tweight,
    )
    got = [
        pltpu.VMEM((HT if dt else td, SUB, LANES if dc else sd), F32) for dt, dc in DIRS
    ]
    dirs = len(DIRS)
    out = pl.pallas_call(
        functools.partial(kernel, nt, nc),
        out_shape=jax.ShapeDtypeStruct((2, covs, td, sd), F32),
        in_specs=[pl.BlockSpec(memory_space=pltpu.HBM)] * len(operands),
        out_specs=pl.BlockSpec(memory_space=pltpu.VMEM),
        scratch_shapes=[pltpu.VMEM(x.shape, x.dtype) for x in operands]
        + [
            pltpu.VMEM((te, SUB, sd), F32),
            pltpu.VMEM((te, SUB, LANES), F32),
            pltpu.VMEM((te, SUB, LANES), F32),
            pltpu.VMEM((2 * cd, sd + LANES), BF16),
            pltpu.VMEM((4 * te * SUB, hd), BF16),
            pltpu.VMEM((hd, 2 * te * SUB), BF16),
            pltpu.VMEM((2 * te * SUB, cd), BF16),
            pltpu.VMEM((te, SUB, sd), F32),
            pltpu.VMEM((te, SUB, LANES), F32),
            got,
            pltpu.SemaphoreType.DMA((8,)),
            pltpu.SemaphoreType.DMA((dirs,)),
            pltpu.SemaphoreType.DMA((dirs,)),
            pltpu.SemaphoreType.DMA((dirs,)),
            pltpu.SemaphoreType.DMA((dirs,)),
        ],
        compiler_params=pltpu.CompilerParams(
            collective_id=0, has_side_effects=True, vmem_limit_bytes=60 * 1024 * 1024
        ),
        name="hessian_product",
    )(*operands)
    out = out.transpose(0, 1, 3, 2)
    return out[0], out[1]


def solution(mesh):
    return jax.shard_map(
        functools.partial(body, mesh.shape["tm"], mesh.shape["cell"]),
        mesh=mesh,
        in_specs=(
            P(None, "cell", "tm"),
            P(None, "cell", "tm"),
            P(None, "cell", "tm"),
            P("cell", "tm"),
            P("cell"),
            P(None, "cell"),
            P("tm"),
            P(None, "tm"),
        ),
        out_specs=(P(None, "cell", "tm"), P(None, "cell", "tm")),
        check_vma=False,
    )
```
